32 devices in a mesh: group: 2 (over y), patch: 4 (over z), tensor: 2 (over x), seq: 2 (over core).
Axes of the slice: x: 2, y: 2, z: 4, core: 2. Of those that a mesh axis runs over, the one named last changes fastest.
Arguments:
- query_raw: bfloat16 [6144, 1536], P(('group', 'patch', 'seq'), 'tensor'), parts along dimension 0, may hold values from -6 to 6
- key_raw: bfloat16 [6144, 1536], P(('group', 'patch', 'seq'), 'tensor'), parts along dimension 0, may hold values from -6 to 6
- value_raw: bfloat16 [6144, 1536], P(('group', 'patch', 'seq'), 'tensor'), parts along dimension 0, may hold values from -6 to 6
- key_cache: bfloat16 [6144, 1536], P(('group', 'patch', 'seq'), 'tensor'), parts along dimension 0, may hold values from -4 to 4
- value_cache: bfloat16 [6144, 1536], P(('group', 'patch', 'seq'), 'tensor'), parts along dimension 0, may hold values from -4 to 4
- norm_gain: float32 [2, 2, 128], replicated, may hold values from 0.5 to 3
- layout: int32 [2, 6144], P(None, ('group', 'patch', 'seq')), parts along dimension 1, may hold values from 0 to 352, as said below
- group_size: int32 [12], P('tensor'), may hold values from 64 to 128, as said below
- step_index: int32 [2], P('group'), parts along dimension 0, may hold values from 0 to 27
- gate_table: float32 [2, 28, 3072], P(None, None, 'seq'), may hold values from -4 to 4
- out_weight: bfloat16 [2, 1536, 3072], P(None, 'tensor', 'seq'), may hold values from -0.15625 to 0.15625
Outputs:
- block_out: bfloat16 [6144, 3072], P(('group', 'patch', 'tensor'), 'seq'), parts along dimension 0
- key_next: bfloat16 [6144, 1536], P(('group', 'patch', 'seq'), 'tensor'), parts along dimension 0
- value_next: bfloat16 [6144, 1536], P(('group', 'patch', 'seq'), 'tensor'), parts along dimension 0
The draws below stay inside these ranges and needn't reach their ends.
There are 2 independent parts, one for each index of `group`. The reference program is written for one: setup_inputs(seed, part) draws one part's arguments, and reference() takes and returns one part's arrays. A program takes and returns all parts, laid end to end along the dimension named above; an argument that names none is the same for every part. Nothing has to cross between parts.
Inputs may be any that keep to these rules, and one draw needn't show every extreme that they name: `layout`: the first 256 tokens (text) have both ids 0; image token j takes row j // w + s and column c + (j % w) or c + w - 1 - (j % w) (one direction for the whole image) of a raster whose width w, 8 to 63, column offset c of at least 1, and direction are drawn for each image, with the row offset s of at least 1 chosen so that the last image token's row is the largest id; no column id exceeds it. `group_size`: each entry is 128 or 64; half of the heads take each.
All inputs are finite; a program needn't handle non-finite values.
Results may differ from the reference program's by a relative error of at most 0.03.
Values may be sent and summed in bfloat16 or wider, within the bound.
A program may use at most 128 MiB of HBM per device.

```python
import math
import jax
import jax.numpy as jnp
from jax import lax

D = 3072
HEADS = 12
RA = 16
RB = 56
STEPS = 28
HD = 128
HH = 1536
TOKENS = 3072
TXT = 256


def draw_layout(key, part):
    key = jax.random.fold_in(key, 7)
    width_key, offset_key, flip_key = jax.random.split(key, 3)
    image_count = TOKENS - TXT
    top_row = (image_count - 1) // 8 + 1
    raster = jax.random.randint(width_key, (), 8, min(64, top_row + 1))
    col_start = jax.random.randint(offset_key, (), 1, top_row - raster + 2)
    flipped = jax.random.randint(flip_key, (), 0, 2)
    image_index = jnp.arange(image_count, dtype=jnp.int32)
    offset = top_row - (image_count - 1) // raster
    rows_id = image_index // raster + offset
    within = image_index % raster
    within = jnp.where(flipped == 1, raster - 1 - within, within)
    cols_id = within + col_start
    zero_text = jnp.zeros((TXT,), jnp.int32)
    return jnp.stack([jnp.concatenate([zero_text, rows_id]), jnp.concatenate([zero_text, cols_id])]).astype(jnp.int32)


def draw_group_size(key, part):
    key = jax.random.fold_in(key, 11)
    shuffled = jax.random.permutation(key, HEADS)
    return jnp.where(shuffled < HEADS // 2, HD, HD // 2).astype(jnp.int32)


def levels(stream_key, extent, cuts, least, largest):
    def one(position, shards_of):
        draws = jax.random.uniform(jax.random.fold_in(jax.random.fold_in(stream_key, 6), position), (shards_of,), jnp.float32, least / len(cuts), largest / len(cuts))
        return jnp.repeat(jnp.exp(draws), extent[position] // shards_of).reshape((-1,) + (1,) * (len(extent) - position - 1))

    level = one(*cuts[0])
    for cut in cuts[1:]:
        level = level * one(*cut)
    return level


def scatter_about(key, extent, scale, bound, cuts=(), kind=jnp.bfloat16):
    values = scale * jax.random.normal(key, extent, jnp.float32)
    if cuts:
        values = values * levels(key, extent, cuts, -0.22, 0.18)
    return jnp.clip(values, -bound, bound).astype(kind)


def setup_inputs(seed: int = 0, part: int = 0) -> dict:
    keys = jax.random.split(jax.random.key(seed), 12)
    part_keys = jax.random.split(jax.random.fold_in(keys[11], part), 12)
    query_raw = scatter_about(part_keys[0], (TOKENS, HH), 1.0, 6.0, ((0, 8), (1, 2)))
    key_raw = scatter_about(part_keys[1], (TOKENS, HH), 1.0, 6.0, ((0, 8), (1, 2)))
    value_raw = scatter_about(part_keys[2], (TOKENS, HH), 1.0, 6.0, ((0, 8), (1, 2)))
    key_cache = scatter_about(part_keys[3], (TOKENS, HH), 1.0, 4.0, ((0, 8), (1, 2)))
    value_cache = scatter_about(part_keys[4], (TOKENS, HH), 1.0, 4.0, ((0, 8), (1, 2)))
    norm_gain = jnp.clip(jnp.exp(jax.random.uniform(keys[5], (2, 2, HD), jnp.float32, math.log(0.5), math.log(3.0))), 0.5, 3.0)
    layout = draw_layout(jax.random.fold_in(jax.random.fold_in(keys[11], part), 71), part)
    group_size = draw_group_size(jax.random.fold_in(keys[11], 71), part)
    step_index = jax.random.randint(part_keys[8], (1,), 0, STEPS).astype(jnp.int32)
    gate_table = scatter_about(keys[9], (2, STEPS, D), 1.0, 4.0, ((2, 2),), jnp.float32)
    out_weight = scatter_about(keys[10], (2, HH, D), HH ** -0.5, 0.15625, ((1, 2), (2, 2)))
    return dict(query_raw=query_raw, key_raw=key_raw, value_raw=value_raw, key_cache=key_cache, value_cache=value_cache, norm_gain=norm_gain, layout=layout, group_size=group_size, step_index=step_index, gate_table=gate_table, out_weight=out_weight)


rope_theta = 10000.0
norm_eps = 1e-06

def rope_tables(positions, plain_dims, rotary_dims):
    half_len = rotary_dims // 2
    exponent = jnp.arange(half_len, dtype=jnp.float32) * (2.0 / rotary_dims)
    freqs = jnp.exp(-jnp.log(rope_theta) * exponent)
    token_count = positions.shape[1]
    cosine = [jnp.ones((token_count, plain_dims), jnp.float32)]
    sine_part = [jnp.zeros((token_count, plain_dims), jnp.float32)]
    for which in range(2):
        angle = positions[which].astype(jnp.float32)[:, None] * freqs[None, :]
        cosine += [jnp.cos(angle), jnp.cos(angle)]
        sine_part += [jnp.sin(angle), jnp.sin(angle)]
    return (jnp.concatenate(cosine, 1), jnp.concatenate(sine_part, 1))

def partner(values, plain_dims, rotary_dims):
    half_len = rotary_dims // 2
    first = plain_dims
    second = plain_dims + rotary_dims
    return jnp.concatenate([values[..., :first], -values[..., first + half_len:second], values[..., first:first + half_len], -values[..., second + half_len:], values[..., second:second + half_len]], -1)

def compress(residual, group_size, heads, head_dim):
    row_count = residual.shape[0]
    halves = residual.reshape(row_count, heads, 2, head_dim // 2)
    half_ms = lax.optimization_barrier(jnp.mean(halves * halves, -1))
    whole_ms = lax.optimization_barrier(jnp.mean(half_ms, -1, keepdims=True))
    whole = (group_size == head_dim)[None, :, None]
    mean_sq = jnp.where(whole, whole_ms, half_ms)
    scales = jnp.sqrt(mean_sq + norm_eps).astype(jnp.bfloat16)
    codes = jnp.tanh(halves / scales.astype(jnp.float32)[..., None]).astype(jnp.bfloat16)
    return (codes.reshape(row_count, heads * head_dim), scales.reshape(row_count, heads * 2))

def decode(codes, scales, heads, head_dim):
    row_count = codes.shape[0]
    parts = codes.astype(jnp.float32).reshape(row_count, heads, 2, head_dim // 2) * scales.astype(jnp.float32).reshape(row_count, heads, 2, 1)
    return parts.reshape(row_count, heads * head_dim)

def prepare(query_raw, key_raw, value_raw, positions, norm_gain, key_rows, value_rows, group_size):
    row_count = query_raw.shape[0]
    heads = group_size.shape[0]
    head_dim = norm_gain.shape[-1]
    text_rows = (positions[0] == 0)[:, None, None]
    cosine, sine_part = rope_tables(positions, RA, RB)
    cosine = cosine[:, None, :]
    sine_part = sine_part[:, None, :]

    def embed(raw, which):
        gain = jnp.where(text_rows, norm_gain[0, which][None, None, :], norm_gain[1, which][None, None, :])
        values = raw.astype(jnp.float32).reshape(row_count, heads, head_dim)
        normed = values * lax.rsqrt(lax.optimization_barrier(jnp.mean(values * values, -1, keepdims=True)) + norm_eps) * gain
        return (normed * cosine + partner(normed, RA, RB) * sine_part).reshape(row_count, heads * head_dim)
    query_rot = embed(query_raw, 0).astype(jnp.bfloat16)
    key_rot = embed(key_raw, 1)
    key_codes, key_scales = compress(key_rot - key_rows.astype(jnp.float32), group_size, heads, head_dim)
    value_codes, value_scales = compress(value_raw.astype(jnp.float32) - value_rows.astype(jnp.float32), group_size, heads, head_dim)
    return (query_rot, key_codes, value_codes, key_scales, value_scales)

def reference(query_raw, key_raw, value_raw, key_cache, value_cache, norm_gain, layout, group_size, step_index, gate_table, out_weight):
    query_rot, key_codes, value_codes, key_scales, value_scales = prepare(query_raw, key_raw, value_raw, layout, norm_gain, key_cache, value_cache, group_size)
    key_next = (key_cache.astype(jnp.float32) + decode(key_codes, key_scales, HEADS, HD)).astype(jnp.bfloat16)
    value_next = (value_cache.astype(jnp.float32) + decode(value_codes, value_scales, HEADS, HD)).astype(jnp.bfloat16)

    def split_heads(values):
        return values.reshape(TOKENS, HEADS, HD).transpose(1, 0, 2)

    def attend(operands):
        query_head, key_head, value_head = operands
        scores = jnp.dot(query_head, key_head.T, preferred_element_type=jnp.float32) * HD ** (-0.5)
        weights = jnp.exp(scores)
        totals = lax.optimization_barrier(jnp.sum(weights, -1, keepdims=True))
        mixed = jnp.dot(weights.astype(jnp.bfloat16), value_head, preferred_element_type=jnp.float32)
        return mixed / totals
    attended = lax.map(attend, (split_heads(query_rot), split_heads(key_next), split_heads(value_next)))
    attn_rows = attended.transpose(1, 0, 2).reshape(TOKENS, HH).astype(jnp.bfloat16)
    text_rows = (layout[0] == 0)[:, None]
    projected = jnp.where(text_rows, jnp.dot(attn_rows, out_weight[0], preferred_element_type=jnp.float32), jnp.dot(attn_rows, out_weight[1], preferred_element_type=jnp.float32))
    gates = gate_table[:, step_index[0]]
    gate_rows = jnp.where(text_rows, gates[0][None, :], gates[1][None, :])
    block_out = (gate_rows * projected).astype(jnp.bfloat16)
    return (block_out, key_next, value_next)
```

```python
import functools
import math
import jax
import jax.numpy as jnp
import numpy as np
from jax import lax
from jax.experimental import pallas as pl
from jax.experimental.pallas import tpu as pltpu
from jax.sharding import PartitionSpec as P

RA = 16
RB = 56


rope_theta = 10000.0
norm_eps = 1e-06


def rope_tables(positions, plain_dims, rotary_dims):
    half_len = rotary_dims // 2
    exponent = jnp.arange(half_len, dtype=jnp.float32) * (2.0 / rotary_dims)
    freqs = jnp.exp(-jnp.log(rope_theta) * exponent)
    token_count = positions.shape[1]
    cosine = [jnp.ones((token_count, plain_dims), jnp.float32)]
    sine_part = [jnp.zeros((token_count, plain_dims), jnp.float32)]
    for which in range(2):
        angle = positions[which].astype(jnp.float32)[:, None] * freqs[None, :]
        cosine += [jnp.cos(angle), jnp.cos(angle)]
        sine_part += [jnp.sin(angle), jnp.sin(angle)]
    return (jnp.concatenate(cosine, 1), jnp.concatenate(sine_part, 1))


def partner(values, plain_dims, rotary_dims):
    half_len = rotary_dims // 2
    second = plain_dims + rotary_dims
    return jnp.concatenate(
        [
            values[..., :plain_dims],
            -values[..., plain_dims + half_len : second],
            values[..., plain_dims : plain_dims + half_len],
            -values[..., second + half_len :],
            values[..., second : second + half_len],
        ],
        -1,
    )


def compress(residual, group_size, heads, head_dim):
    row_count = residual.shape[0]
    halves = residual.reshape(row_count, heads, 2, head_dim // 2)
    half_ms = jnp.mean(halves * halves, -1)
    whole_ms = jnp.mean(half_ms, -1, keepdims=True)
    whole = (group_size == head_dim)[None, :, None]
    mean_sq = jnp.where(whole, whole_ms, half_ms)
    scales = jnp.sqrt(mean_sq + norm_eps).astype(jnp.bfloat16)
    codes = jnp.tanh(halves / scales.astype(jnp.float32)[..., None]).astype(jnp.bfloat16)
    return (codes.reshape(row_count, heads * head_dim), scales.reshape(row_count, heads * 2))


def decode(codes, scales, heads, head_dim):
    row_count = codes.shape[0]
    parts = codes.astype(jnp.float32).reshape(row_count, heads, 2, head_dim // 2) * scales.astype(
        jnp.float32
    ).reshape(row_count, heads, 2, 1)
    return parts.reshape(row_count, heads * head_dim)


def prepare(query_raw, key_raw, value_raw, positions, norm_gain, key_rows, value_rows, group_size):
    row_count = query_raw.shape[0]
    heads = group_size.shape[0]
    head_dim = norm_gain.shape[-1]
    text_rows = (positions[0] == 0)[:, None, None]
    cosine, sine_part = rope_tables(positions, RA, RB)
    cosine = cosine[:, None, :]
    sine_part = sine_part[:, None, :]

    def embed(raw, which):
        gain = jnp.where(
            text_rows, norm_gain[0, which][None, None, :], norm_gain[1, which][None, None, :]
        )
        values = raw.astype(jnp.float32).reshape(row_count, heads, head_dim)
        normed = values * lax.rsqrt(jnp.mean(values * values, -1, keepdims=True) + norm_eps) * gain
        return (normed * cosine + partner(normed, RA, RB) * sine_part).reshape(
            row_count, heads * head_dim
        )

    query_rot = embed(query_raw, 0).astype(jnp.bfloat16)
    key_rot = embed(key_raw, 1)
    key_codes, key_scales = compress(
        key_rot - key_rows.astype(jnp.float32), group_size, heads, head_dim
    )
    value_codes, value_scales = compress(
        value_raw.astype(jnp.float32) - value_rows.astype(jnp.float32), group_size, heads, head_dim
    )
    return (query_rot, key_codes, value_codes, key_scales, value_scales)


def block_length(piece_rows):
    for candidate in range(min(piece_rows, 2048), 0, -1):
        if piece_rows % candidate == 0:
            return candidate
    return piece_rows


def on_device(
    query_raw,
    key_raw,
    value_raw,
    key_cache,
    value_cache,
    norm_gain,
    layout,
    group_size,
    step_index,
    gate_table,
    out_weight,
):
    row_count = query_raw.shape[0]
    heads = group_size.shape[0]
    head_dim = norm_gain.shape[-1]
    query_rot, key_codes, value_codes, key_scales, value_scales = prepare(
        query_raw, key_raw, value_raw, layout, norm_gain, key_cache, value_cache, group_size
    )
    key_mine = (
        key_cache.astype(jnp.float32) + decode(key_codes, key_scales, heads, head_dim)
    ).astype(jnp.bfloat16)
    value_mine = (
        value_cache.astype(jnp.float32) + decode(value_codes, value_scales, heads, head_dim)
    ).astype(jnp.bfloat16)
    query_heads = query_rot.reshape(row_count, heads, head_dim)
    inverse_root = head_dim ** (-0.5)
    start_state = (
        jnp.zeros((heads, row_count, head_dim), jnp.float32),
        jnp.zeros((heads, row_count), jnp.float32),
    )
    keys_all = lax.all_gather(key_mine, ("patch", "seq"), axis=0, tiled=True)
    values_all = lax.all_gather(value_mine, ("patch", "seq"), axis=0, tiled=True)
    piece_rows = keys_all.shape[0]
    length = block_length(piece_rows)

    def one_block(index, carry):
        numer, totals = carry
        keys = lax.dynamic_slice_in_dim(keys_all, index * length, length, 0).reshape(
            length, heads, head_dim
        )
        values = lax.dynamic_slice_in_dim(values_all, index * length, length, 0).reshape(
            length, heads, head_dim
        )
        scores = (
            jnp.einsum("qhd,khd->hqk", query_heads, keys, preferred_element_type=jnp.float32)
            * inverse_root
        )
        weights = jnp.exp(scores)
        totals = totals + jnp.sum(weights, -1)
        numer = numer + jnp.einsum(
            "hqk,khd->hqd", weights.astype(jnp.bfloat16), values, preferred_element_type=jnp.float32
        )
        return (numer, totals)

    numer, totals = lax.fori_loop(0, piece_rows // length, one_block, start_state)
    attn_rows = (
        (numer / totals[..., None])
        .transpose(1, 0, 2)
        .reshape(row_count, heads * head_dim)
        .astype(jnp.bfloat16)
    )
    text_flag = (layout[0] == 0).astype(jnp.bfloat16)
    pair_attn, pair_text = (
        lax.all_gather(attn_rows, "seq", axis=0, tiled=True),
        lax.all_gather(text_flag, "seq", axis=0, tiled=True),
    )
    share = pair_attn.shape[0] // lax.axis_size("tensor")

    def both_streams(block, block_text):
        text_part = jnp.dot(block, out_weight[0], preferred_element_type=jnp.float32)
        image_part = jnp.dot(block, out_weight[1], preferred_element_type=jnp.float32)
        return jnp.where(block_text[:, None] > 0, text_part, image_part)

    def image_only(block, block_text):
        return jnp.dot(block, out_weight[1], preferred_element_type=jnp.float32)

    block = pair_attn
    block_text = pair_text
    projected = lax.psum_scatter(
        lax.cond(jnp.any(block_text > 0), both_streams, image_only, block, block_text),
        "tensor",
        scatter_dimension=0,
        tiled=True,
    )
    mine_text = lax.dynamic_slice_in_dim(pair_text, lax.axis_index("tensor") * share, share, 0)
    chosen = (jnp.arange(gate_table.shape[1]) == step_index[0]).astype(jnp.float32)
    gates = jnp.sum(gate_table * chosen[None, :, None], 1)
    gate_rows = jnp.where(mine_text[:, None] > 0, gates[0][None, :], gates[1][None, :])
    return ((gate_rows * projected).astype(jnp.bfloat16), key_mine, value_mine)


MESH = pl.DeviceIdType.MESH
GATHER_SHARE = 2


def lane_tables(head_dim):
    half_len = RB // 2
    freqs = np.exp(-math.log(rope_theta) * np.arange(half_len) * (2.0 / RB)).astype(np.float32)
    table = np.zeros((8, head_dim), np.float32)
    for which in range(2):
        start = RA + which * RB
        table[which, start : start + half_len] = freqs
        table[which, start + half_len : start + RB] = freqs
        table[2, start : start + half_len] = -1.0
        table[3, start + half_len : start + RB] = 1.0
    return jnp.asarray(table)


def split_dot(values, matrix):
    high = values.astype(jnp.bfloat16)
    low = (values - high.astype(jnp.float32)).astype(jnp.bfloat16)
    return jnp.dot(
        jnp.concatenate([high, low], 1),
        jnp.concatenate([matrix, matrix], 0),
        preferred_element_type=jnp.float32,
    )


def prepare_kernel(
    sizes, positions, gains, table, query, key, value, key_old, value_old,
    query_out, pair_out, key_out, value_out, cosine, sine_low, sine_high, gain_q, gain_k,
):
    head = pl.program_id(0)
    head_dim = query.shape[1]
    half_len = RB // 2

    @pl.when(head == 0)
    def _():
        rows_id = positions[:, 0:1]
        angle = rows_id * table[0:1, :] + positions[:, 1:2] * table[1:2, :]
        sine = jnp.sin(angle)
        cosine[...] = jnp.cos(angle)
        sine_low[...] = sine * table[2:3, :]
        sine_high[...] = sine * table[3:4, :]
        text = rows_id == 0
        gain_q[...] = jnp.where(text, gains[0:1, :], gains[2:3, :])
        gain_k[...] = jnp.where(text, gains[1:2, :], gains[3:4, :])

    full = jnp.full((head_dim, head_dim), 1.0 / head_dim, jnp.float32)
    row = lax.broadcasted_iota(jnp.int32, (head_dim, head_dim), 0) < head_dim // 2
    col = lax.broadcasted_iota(jnp.int32, (head_dim, head_dim), 1) < head_dim // 2
    halves = jnp.where(row == col, 2.0 / head_dim, 0.0)
    whole = (sizes[head] == head_dim).astype(jnp.float32)
    grouped = (whole * full + (1.0 - whole) * halves).astype(jnp.bfloat16)
    full = full.astype(jnp.bfloat16)

    def embed(raw, gain):
        values = raw[...].astype(jnp.float32)
        normed = values * lax.rsqrt(split_dot(values * values, full) + norm_eps) * gain[...]
        return (
            normed * cosine[...]
            + pltpu.roll(normed, head_dim - half_len, 1) * sine_low[...]
            + pltpu.roll(normed, half_len, 1) * sine_high[...]
        )

    def update(fresh, old):
        kept = old[...].astype(jnp.float32)
        residual = fresh - kept
        scale = jnp.sqrt(split_dot(residual * residual, grouped) + norm_eps)
        scale = scale.astype(jnp.bfloat16).astype(jnp.float32)
        code = jnp.tanh(residual / scale).astype(jnp.bfloat16).astype(jnp.float32)
        return (kept + scale * code).astype(jnp.bfloat16)

    query_out[0] = embed(query, gain_q).astype(jnp.bfloat16)
    key_next = update(embed(key, gain_k), key_old)
    value_next = update(value[...].astype(jnp.float32), value_old)
    pair_out[0, 0] = key_next
    pair_out[0, 1] = value_next
    key_out[...] = key_next
    value_out[...] = value_next


def prepare_call(query, key, value, key_old, value_old, norm_gain, layout, group_size):
    rows, width = query.shape
    heads = group_size.shape[0]
    hd = width // heads
    block = pl.BlockSpec((rows, hd), lambda h: (0, h))
    whole = lambda *shape: pl.BlockSpec(shape, lambda h: (0,) * len(shape))
    return pl.pallas_call(
        prepare_kernel,
        grid=(heads,),
        in_specs=[
            pl.BlockSpec(memory_space=pltpu.SMEM),
            whole(rows, 2),
            whole(4, hd),
            whole(8, hd),
        ]
        + [block] * 5,
        out_specs=[
            pl.BlockSpec((1, rows, hd), lambda h: (h, 0, 0)),
            pl.BlockSpec((1, 2, rows, hd), lambda h: (h, 0, 0, 0)),
            block,
            block,
        ],
        out_shape=[
            jax.ShapeDtypeStruct((heads, rows, hd), jnp.bfloat16),
            jax.ShapeDtypeStruct((heads, 2, rows, hd), jnp.bfloat16),
            jax.ShapeDtypeStruct((rows, width), jnp.bfloat16),
            jax.ShapeDtypeStruct((rows, width), jnp.bfloat16),
        ],
        scratch_shapes=[pltpu.VMEM((rows, hd), jnp.float32)] * 5,
        compiler_params=pltpu.CompilerParams(vmem_limit_bytes=32 * 2**20),
    )(
        group_size,
        layout.astype(jnp.float32).T,
        norm_gain.reshape(4, hd),
        lane_tables(hd),
        query,
        key,
        value,
        key_old,
        value_old,
    )


def attend_kernel(
    query, pair, out, held, guest, mixed, returned, in_send, out_send, side_send, line_recv,
    side_recv, guest_send, guest_recv, back_send, back_recv,
):
    heads, rows, hd = query.shape
    shared = heads // GATHER_SHARE
    chip = lax.axis_index("patch")
    core = lax.axis_index("seq")
    other_core = 1 - core
    upper = chip // 2
    is_end = (chip == 0) | (chip == 3)
    is_mid = jnp.logical_not(is_end)
    my_end = upper * 3
    my_mid = 1 + upper
    far_mid = 2 - upper
    far_end = 3 - my_end
    inner = jnp.where(is_end, my_mid, far_mid)
    outer = my_end

    def slot(source):
        return source * 2 + core

    def to_chip(src, dst, send, recv, target):
        return pltpu.make_async_remote_copy(
            src_ref=src, dst_ref=dst, send_sem=send, recv_sem=recv,
            device_id={"patch": target}, device_id_type=MESH,
        )

    def along(h, source, target, send):
        where = held.at[h, slot(source)]
        return to_chip(where, where, send.at[h, source], line_recv.at[h, source], target)

    def aside(h, source):
        where = held.at[h, slot(source)]
        return pltpu.make_async_remote_copy(
            src_ref=where, dst_ref=where, send_sem=side_send.at[h, source],
            recv_sem=side_recv.at[h, source],
            device_id={"seq": other_core}, device_id_type=MESH,
        )

    def lend(h):
        return to_chip(
            query.at[h], guest.at[h], guest_send.at[h], guest_recv.at[h], inner
        )

    def give_back(h):
        return to_chip(
            mixed.at[h], returned.at[h], back_send.at[h], back_recv.at[h], outer
        )

    factor = hd ** (-0.5) * math.log2(math.e)
    ones = jnp.ones((rows, hd), jnp.bfloat16)

    def attend(rows_q, h):
        def one(source, total):
            keys = held[h, source, 0]
            values = jnp.concatenate([held[h, source, 1], ones], 1)
            scores = lax.dot_general(
                rows_q, keys, (((1,), (1,)), ((), ())), preferred_element_type=jnp.float32
            )
            weights = jnp.exp2(scores * factor).astype(jnp.bfloat16)
            return total + jnp.dot(weights, values, preferred_element_type=jnp.float32)

        total = lax.fori_loop(0, 8, one, jnp.zeros((rows, 2 * hd), jnp.float32))
        return (total[:, :hd] / total[:, hd:]).astype(jnp.bfloat16)

    barrier = pltpu.get_barrier_semaphore()
    pl.semaphore_signal(barrier, inc=1, device_id={"seq": other_core}, device_id_type=MESH)
    pl.semaphore_signal(barrier, inc=1, device_id={"patch": inner}, device_id_type=MESH)

    @pl.when(is_mid)
    def _():
        pl.semaphore_signal(barrier, inc=1, device_id={"patch": outer}, device_id_type=MESH)

    pl.semaphore_wait(barrier, jnp.where(is_end, 2, 3))

    def arrived(h, source):
        along(h, source, inner, in_send).wait_recv()

    def siblings(h):
        def one(source, carry):
            aside(h, source).wait_recv()
            return carry

        lax.fori_loop(0, 4, one, 0)

    def store_own(h, carry):
        held[h, slot(chip)] = pair[h]
        return carry

    lax.fori_loop(0, heads, store_own, 0)

    @pl.when(is_end)
    def _():
        def push(h, carry):
            along(h, chip, inner, in_send).start()

            @pl.when(h < shared)
            def _():
                aside(h, chip).start()

            @pl.when(h >= shared)
            def _():
                lend(h).start()

            return carry

        lax.fori_loop(0, heads, push, 0)

        def step(h, carry):
            for source in (my_mid, far_mid, far_end):
                arrived(h, source)
                aside(h, source).start()
            siblings(h)
            returned[h] = attend(query[h], h)
            return carry

        lax.fori_loop(0, shared, step, 0)

        def finish(h, carry):
            give_back(h).wait_recv()
            return carry

        lax.fori_loop(shared, heads, finish, 0)

        def drain(h, carry):
            along(h, chip, inner, in_send).wait_send()

            @pl.when(h < shared)
            def _():
                for source in (chip, my_mid, far_mid, far_end):
                    aside(h, source).wait_send()

            @pl.when(h >= shared)
            def _():
                lend(h).wait_send()

            return carry

        lax.fori_loop(0, heads, drain, 0)

    @pl.when(is_mid)
    def _():
        def push(h, carry):
            @pl.when(h < 2)
            def _():
                along(h, chip, inner, in_send).start()

            @pl.when(h < shared)
            def _():
                along(h, chip, outer, out_send).start()

            aside(h, chip).start()
            return carry

        lax.fori_loop(0, heads, push, 0)

        def take_end(h):
            arrived(h, my_end)
            along(h, my_end, inner, in_send).start()
            aside(h, my_end).start()

        take_end(0)

        def step(h, carry):
            @pl.when(h + 2 < heads)
            def _():
                along(h + 2, chip, inner, in_send).start()

            @pl.when(h + 1 < heads)
            def _():
                take_end(h + 1)

            for source in (far_mid, far_end):
                arrived(h, source)
                aside(h, source).start()

                @pl.when(h < shared)
                def _():
                    along(h, source, outer, out_send).start()

            siblings(h)

            @pl.when(h >= shared)
            def _():
                lend(h).wait_recv()
                mixed[h] = attend(guest[h], h)
                give_back(h).start()

            returned[h] = attend(query[h], h)
            return carry

        lax.fori_loop(0, heads, step, 0)

        def drain(h, carry):
            along(h, chip, inner, in_send).wait_send()
            along(h, my_end, inner, in_send).wait_send()
            for source in (chip, my_end, far_mid, far_end):
                aside(h, source).wait_send()

            @pl.when(h < shared)
            def _():
                for source in (chip, far_mid, far_end):
                    along(h, source, outer, out_send).wait_send()

            @pl.when(h >= shared)
            def _():
                give_back(h).wait_send()

            return carry

        lax.fori_loop(0, heads, drain, 0)

    for h in range(heads):
        out[:, h * hd : (h + 1) * hd] = returned[h]


def attend_call(query, pair):
    heads, rows, hd = query.shape
    dma = pltpu.SemaphoreType.DMA
    vmem = lambda *shape: pltpu.VMEM(shape, jnp.bfloat16)
    return pl.pallas_call(
        attend_kernel,
        out_shape=jax.ShapeDtypeStruct((rows, heads * hd), jnp.bfloat16),
        in_specs=[pl.BlockSpec(memory_space=pltpu.VMEM)] * 2,
        out_specs=pl.BlockSpec(memory_space=pltpu.VMEM),
        scratch_shapes=[
            vmem(heads, 8, 2, rows, hd),
            vmem(heads, rows, hd),
            vmem(heads, rows, hd),
            vmem(heads, rows, hd),
        ]
        + [dma((heads, 4))] * 5
        + [dma((heads,))] * 4,
        compiler_params=pltpu.CompilerParams(
            collective_id=0, has_side_effects=True, vmem_limit_bytes=48 * 2**20
        ),
    )(query, pair)


def on_device_line(
    query_raw,
    key_raw,
    value_raw,
    key_cache,
    value_cache,
    norm_gain,
    layout,
    group_size,
    step_index,
    gate_table,
    out_weight,
):
    query_rot, pair, key_mine, value_mine = prepare_call(
        query_raw, key_raw, value_raw, key_cache, value_cache, norm_gain, layout, group_size
    )
    attn_rows = attend_call(query_rot, pair)
    text_flag = (layout[0] == 0).astype(jnp.bfloat16)
    pair_attn = lax.all_gather(attn_rows, "seq", axis=0, tiled=True)
    pair_text = lax.all_gather(text_flag, "seq", axis=0, tiled=True)
    share = pair_attn.shape[0] // 2

    def both_streams(block, block_text):
        text_part = jnp.dot(block, out_weight[0], preferred_element_type=jnp.float32)
        image_part = jnp.dot(block, out_weight[1], preferred_element_type=jnp.float32)
        return jnp.where(block_text[:, None] > 0, text_part, image_part)

    def image_only(block, block_text):
        return jnp.dot(block, out_weight[1], preferred_element_type=jnp.float32)

    partial = lax.cond(
        jnp.any(pair_text > 0), both_streams, image_only, pair_attn, pair_text
    )
    mine = lax.axis_index("tensor")
    kept = lax.dynamic_slice_in_dim(partial, mine * share, share, 0)
    sent = lax.dynamic_slice_in_dim(partial, (1 - mine) * share, share, 0).astype(jnp.bfloat16)
    got = lax.ppermute(sent, "tensor", [(0, 1), (1, 0)])
    projected = kept + got.astype(jnp.float32)
    mine_text = lax.dynamic_slice_in_dim(pair_text, mine * share, share, 0)
    chosen = (jnp.arange(gate_table.shape[1]) == step_index[0]).astype(jnp.float32)
    gates = jnp.sum(gate_table * chosen[None, :, None], 1)
    gate_rows = jnp.where(mine_text[:, None] > 0, gates[0][None, :], gates[1][None, :])
    return ((gate_rows * projected).astype(jnp.bfloat16), key_mine, value_mine)


def solution(mesh):
    in_specs = (
        P(("group", "patch", "seq"), "tensor"),
        P(("group", "patch", "seq"), "tensor"),
        P(("group", "patch", "seq"), "tensor"),
        P(("group", "patch", "seq"), "tensor"),
        P(("group", "patch", "seq"), "tensor"),
        P(),
        P(None, ("group", "patch", "seq")),
        P("tensor"),
        P("group"),
        P(None, None, "seq"),
        P(None, "tensor", "seq"),
    )
    out_specs = (
        P(("group", "patch", "tensor"), "seq"),
        P(("group", "patch", "seq"), "tensor"),
        P(("group", "patch", "seq"), "tensor"),
    )
    fast = mesh.shape["patch"] == 4 and mesh.shape["tensor"] == 2 and mesh.shape["seq"] == 2
    return jax.shard_map(
        on_device_line if fast else on_device, mesh=mesh, in_specs=in_specs, out_specs=out_specs, check_vma=False
    )
```

```python
import functools
import math
import jax
import jax.numpy as jnp
import numpy as np
from jax import lax
from jax.experimental import pallas as pl
from jax.experimental.pallas import tpu as pltpu
from jax.sharding import PartitionSpec as P

RA = 16
RB = 56


rope_theta = 10000.0
norm_eps = 1e-06


def rope_tables(positions, plain_dims, rotary_dims):
    half_len = rotary_dims // 2
    exponent = jnp.arange(half_len, dtype=jnp.float32) * (2.0 / rotary_dims)
    freqs = jnp.exp(-jnp.log(rope_theta) * exponent)
    token_count = positions.shape[1]
    cosine = [jnp.ones((token_count, plain_dims), jnp.float32)]
    sine_part = [jnp.zeros((token_count, plain_dims), jnp.float32)]
    for which in range(2):
        angle = positions[which].astype(jnp.float32)[:, None] * freqs[None, :]
        cosine += [jnp.cos(angle), jnp.cos(angle)]
        sine_part += [jnp.sin(angle), jnp.sin(angle)]
    return (jnp.concatenate(cosine, 1), jnp.concatenate(sine_part, 1))


def partner(values, plain_dims, rotary_dims):
    half_len = rotary_dims // 2
    second = plain_dims + rotary_dims
    return jnp.concatenate(
        [
            values[..., :plain_dims],
            -values[..., plain_dims + half_len : second],
            values[..., plain_dims : plain_dims + half_len],
            -values[..., second + half_len :],
            values[..., second : second + half_len],
        ],
        -1,
    )


def compress(residual, group_size, heads, head_dim):
    row_count = residual.shape[0]
    halves = residual.reshape(row_count, heads, 2, head_dim // 2)
    half_ms = jnp.mean(halves * halves, -1)
    whole_ms = jnp.mean(half_ms, -1, keepdims=True)
    whole = (group_size == head_dim)[None, :, None]
    mean_sq = jnp.where(whole, whole_ms, half_ms)
    scales = jnp.sqrt(mean_sq + norm_eps).astype(jnp.bfloat16)
    codes = jnp.tanh(halves / scales.astype(jnp.float32)[..., None]).astype(jnp.bfloat16)
    return (codes.reshape(row_count, heads * head_dim), scales.reshape(row_count, heads * 2))


def decode(codes, scales, heads, head_dim):
    row_count = codes.shape[0]
    parts = codes.astype(jnp.float32).reshape(row_count, heads, 2, head_dim // 2) * scales.astype(
        jnp.float32
    ).reshape(row_count, heads, 2, 1)
    return parts.reshape(row_count, heads * head_dim)


def prepare(query_raw, key_raw, value_raw, positions, norm_gain, key_rows, value_rows, group_size):
    row_count = query_raw.shape[0]
    heads = group_size.shape[0]
    head_dim = norm_gain.shape[-1]
    text_rows = (positions[0] == 0)[:, None, None]
    cosine, sine_part = rope_tables(positions, RA, RB)
    cosine = cosine[:, None, :]
    sine_part = sine_part[:, None, :]

    def embed(raw, which):
        gain = jnp.where(
            text_rows, norm_gain[0, which][None, None, :], norm_gain[1, which][None, None, :]
        )
        values = raw.astype(jnp.float32).reshape(row_count, heads, head_dim)
        normed = values * lax.rsqrt(jnp.mean(values * values, -1, keepdims=True) + norm_eps) * gain
        return (normed * cosine + partner(normed, RA, RB) * sine_part).reshape(
            row_count, heads * head_dim
        )

    query_rot = embed(query_raw, 0).astype(jnp.bfloat16)
    key_rot = embed(key_raw, 1)
    key_codes, key_scales = compress(
        key_rot - key_rows.astype(jnp.float32), group_size, heads, head_dim
    )
    value_codes, value_scales = compress(
        value_raw.astype(jnp.float32) - value_rows.astype(jnp.float32), group_size, heads, head_dim
    )
    return (query_rot, key_codes, value_codes, key_scales, value_scales)


def block_length(piece_rows):
    for candidate in range(min(piece_rows, 2048), 0, -1):
        if piece_rows % candidate == 0:
            return candidate
    return piece_rows


def on_device(
    query_raw,
    key_raw,
    value_raw,
    key_cache,
    value_cache,
    norm_gain,
    layout,
    group_size,
    step_index,
    gate_table,
    out_weight,
):
    row_count = query_raw.shape[0]
    heads = group_size.shape[0]
    head_dim = norm_gain.shape[-1]
    query_rot, key_codes, value_codes, key_scales, value_scales = prepare(
        query_raw, key_raw, value_raw, layout, norm_gain, key_cache, value_cache, group_size
    )
    key_mine = (
        key_cache.astype(jnp.float32) + decode(key_codes, key_scales, heads, head_dim)
    ).astype(jnp.bfloat16)
    value_mine = (
        value_cache.astype(jnp.float32) + decode(value_codes, value_scales, heads, head_dim)
    ).astype(jnp.bfloat16)
    query_heads = query_rot.reshape(row_count, heads, head_dim)
    inverse_root = head_dim ** (-0.5)
    start_state = (
        jnp.zeros((heads, row_count, head_dim), jnp.float32),
        jnp.zeros((heads, row_count), jnp.float32),
    )
    keys_all = lax.all_gather(key_mine, ("patch", "seq"), axis=0, tiled=True)
    values_all = lax.all_gather(value_mine, ("patch", "seq"), axis=0, tiled=True)
    piece_rows = keys_all.shape[0]
    length = block_length(piece_rows)

    def one_block(index, carry):
        numer, totals = carry
        keys = lax.dynamic_slice_in_dim(keys_all, index * length, length, 0).reshape(
            length, heads, head_dim
        )
        values = lax.dynamic_slice_in_dim(values_all, index * length, length, 0).reshape(
            length, heads, head_dim
        )
        scores = (
            jnp.einsum("qhd,khd->hqk", query_heads, keys, preferred_element_type=jnp.float32)
            * inverse_root
        )
        weights = jnp.exp(scores)
        totals = totals + jnp.sum(weights, -1)
        numer = numer + jnp.einsum(
            "hqk,khd->hqd", weights.astype(jnp.bfloat16), values, preferred_element_type=jnp.float32
        )
        return (numer, totals)

    numer, totals = lax.fori_loop(0, piece_rows // length, one_block, start_state)
    attn_rows = (
        (numer / totals[..., None])
        .transpose(1, 0, 2)
        .reshape(row_count, heads * head_dim)
        .astype(jnp.bfloat16)
    )
    text_flag = (layout[0] == 0).astype(jnp.bfloat16)
    pair_attn, pair_text = (
        lax.all_gather(attn_rows, "seq", axis=0, tiled=True),
        lax.all_gather(text_flag, "seq", axis=0, tiled=True),
    )
    share = pair_attn.shape[0] // lax.axis_size("tensor")

    def both_streams(block, block_text):
        text_part = jnp.dot(block, out_weight[0], preferred_element_type=jnp.float32)
        image_part = jnp.dot(block, out_weight[1], preferred_element_type=jnp.float32)
        return jnp.where(block_text[:, None] > 0, text_part, image_part)

    def image_only(block, block_text):
        return jnp.dot(block, out_weight[1], preferred_element_type=jnp.float32)

    block = pair_attn
    block_text = pair_text
    projected = lax.psum_scatter(
        lax.cond(jnp.any(block_text > 0), both_streams, image_only, block, block_text),
        "tensor",
        scatter_dimension=0,
        tiled=True,
    )
    mine_text = lax.dynamic_slice_in_dim(pair_text, lax.axis_index("tensor") * share, share, 0)
    chosen = (jnp.arange(gate_table.shape[1]) == step_index[0]).astype(jnp.float32)
    gates = jnp.sum(gate_table * chosen[None, :, None], 1)
    gate_rows = jnp.where(mine_text[:, None] > 0, gates[0][None, :], gates[1][None, :])
    return ((gate_rows * projected).astype(jnp.bfloat16), key_mine, value_mine)


MESH = pl.DeviceIdType.MESH
GATHER_SHARE = 2
CHUNKS = 3
TEXT_PART = 12


def lane_tables(head_dim):
    half_len = RB // 2
    freqs = np.exp(-math.log(rope_theta) * np.arange(half_len) * (2.0 / RB)).astype(np.float32)
    table = np.zeros((8, head_dim), np.float32)
    for which in range(2):
        start = RA + which * RB
        table[which, start : start + half_len] = freqs
        table[which, start + half_len : start + RB] = freqs
        table[2, start : start + half_len] = -1.0
        table[3, start + half_len : start + RB] = 1.0
    return jnp.asarray(table)


def split_dot(values, matrix):
    high = values.astype(jnp.bfloat16)
    low = (values - high.astype(jnp.float32)).astype(jnp.bfloat16)
    return jnp.dot(
        jnp.concatenate([high, low], 1),
        jnp.concatenate([matrix, matrix], 0),
        preferred_element_type=jnp.float32,
    )


def prepare_kernel(
    sizes, positions, gains, table, query, key, value, key_old, value_old,
    query_out, pair_out, key_out, value_out, cosine, sine_low, sine_high, gain_q, gain_k,
):
    head = pl.program_id(0)
    head_dim = query.shape[1]
    half_len = RB // 2

    @pl.when(head == 0)
    def _():
        rows_id = positions[:, 0:1]
        angle = rows_id * table[0:1, :] + positions[:, 1:2] * table[1:2, :]
        sine = jnp.sin(angle)
        cosine[...] = jnp.cos(angle)
        sine_low[...] = sine * table[2:3, :]
        sine_high[...] = sine * table[3:4, :]
        text = rows_id == 0
        gain_q[...] = jnp.where(text, gains[0:1, :], gains[2:3, :])
        gain_k[...] = jnp.where(text, gains[1:2, :], gains[3:4, :])

    full = jnp.full((head_dim, head_dim), 1.0 / head_dim, jnp.float32)
    row = lax.broadcasted_iota(jnp.int32, (head_dim, head_dim), 0) < head_dim // 2
    col = lax.broadcasted_iota(jnp.int32, (head_dim, head_dim), 1) < head_dim // 2
    halves = jnp.where(row == col, 2.0 / head_dim, 0.0)
    whole = (sizes[head] == head_dim).astype(jnp.float32)
    grouped = (whole * full + (1.0 - whole) * halves).astype(jnp.bfloat16)
    full = full.astype(jnp.bfloat16)

    def embed(raw, gain):
        values = raw[...].astype(jnp.float32)
        normed = values * lax.rsqrt(split_dot(values * values, full) + norm_eps) * gain[...]
        return (
            normed * cosine[...]
            + pltpu.roll(normed, head_dim - half_len, 1) * sine_low[...]
            + pltpu.roll(normed, half_len, 1) * sine_high[...]
        )

    def update(fresh, old):
        kept = old[...].astype(jnp.float32)
        residual = fresh - kept
        scale = jnp.sqrt(split_dot(residual * residual, grouped) + norm_eps)
        scale = scale.astype(jnp.bfloat16).astype(jnp.float32)
        code = jnp.tanh(residual / scale).astype(jnp.bfloat16).astype(jnp.float32)
        return (kept + scale * code).astype(jnp.bfloat16)

    query_out[0] = embed(query, gain_q).astype(jnp.bfloat16)
    key_next = update(embed(key, gain_k), key_old)
    value_next = update(value[...].astype(jnp.float32), value_old)
    pair_out[0, 0] = key_next
    pair_out[0, 1] = value_next
    key_out[...] = key_next
    value_out[...] = value_next


def prepare_call(query, key, value, key_old, value_old, norm_gain, layout, group_size):
    rows, width = query.shape
    heads = group_size.shape[0]
    hd = width // heads
    block = pl.BlockSpec((rows, hd), lambda h: (0, h))
    whole = lambda *shape: pl.BlockSpec(shape, lambda h: (0,) * len(shape))
    return pl.pallas_call(
        prepare_kernel,
        grid=(heads,),
        in_specs=[
            pl.BlockSpec(memory_space=pltpu.SMEM),
            whole(rows, 2),
            whole(4, hd),
            whole(8, hd),
        ]
        + [block] * 5,
        out_specs=[
            pl.BlockSpec((1, rows, hd), lambda h: (h, 0, 0)),
            pl.BlockSpec((1, 2, rows, hd), lambda h: (h, 0, 0, 0)),
            block,
            block,
        ],
        out_shape=[
            jax.ShapeDtypeStruct((heads, rows, hd), jnp.bfloat16),
            jax.ShapeDtypeStruct((heads, 2, rows, hd), jnp.bfloat16),
            jax.ShapeDtypeStruct((rows, width), jnp.bfloat16),
            jax.ShapeDtypeStruct((rows, width), jnp.bfloat16),
        ],
        scratch_shapes=[pltpu.VMEM((rows, hd), jnp.float32)] * 5,
        compiler_params=pltpu.CompilerParams(vmem_limit_bytes=60 * 2**20),
    )(
        group_size,
        layout.astype(jnp.float32).T,
        norm_gain.reshape(4, hd),
        lane_tables(hd),
        query,
        key,
        value,
        key_old,
        value_old,
    )


def attend_kernel(
    query, pair, gates, weight, out, held, guest, mixed, returned, full, own_weight, far_weight,
    in_send, out_send, side_send, line_recv, side_recv, guest_send, guest_recv, back_send,
    back_recv, full_send, full_recv, across_send, across_recv, group_send, group_recv, load_sem,
):
    heads, rows, hd = query.shape
    features, columns = weight.shape[1:]
    group = lax.axis_index("group")
    side = lax.axis_index("tensor")
    shared = heads // GATHER_SHARE
    chip = lax.axis_index("patch")
    core = lax.axis_index("seq")
    other_core = 1 - core
    upper = chip // 2
    is_end = (chip == 0) | (chip == 3)
    is_mid = jnp.logical_not(is_end)
    my_end = upper * 3
    my_mid = 1 + upper
    far_mid = 2 - upper
    far_end = 3 - my_end
    inner = jnp.where(is_end, my_mid, far_mid)
    outer = my_end

    def slot(source):
        return source * 2 + core

    def to_chip(src, dst, send, recv, target):
        return pltpu.make_async_remote_copy(
            src_ref=src, dst_ref=dst, send_sem=send, recv_sem=recv,
            device_id={"patch": target}, device_id_type=MESH,
        )

    def along(h, source, target, send):
        where = held.at[h, slot(source)]
        return to_chip(where, where, send.at[h, source], line_recv.at[h, source], target)

    def aside(h, source):
        where = held.at[h, slot(source)]
        return pltpu.make_async_remote_copy(
            src_ref=where, dst_ref=where, send_sem=side_send.at[h, source],
            recv_sem=side_recv.at[h, source],
            device_id={"seq": other_core}, device_id_type=MESH,
        )

    def lend(h):
        return to_chip(
            query.at[h], guest.at[h], guest_send.at[h], guest_recv.at[h], inner
        )

    def give_back(h):
        return to_chip(
            mixed.at[h], returned.at[h], back_send.at[h], back_recv.at[h], outer
        )

    has_text = (chip == 0) & (side == 0)
    gives_text = (chip == 0) & (side == 1)
    text_rows = rows * 8 // TEXT_PART
    chunk = features // 2 // CHUNKS

    def weight_rows(owner, c):
        return pl.ds(pl.multiple_of(owner * (features // 2) + c * chunk, chunk), chunk)

    def across(stream, c):
        where = weight_rows(group, c)
        return pltpu.make_async_remote_copy(
            src_ref=weight.at[stream, where], dst_ref=far_weight.at[stream, where],
            send_sem=across_send.at[stream, c], recv_sem=across_recv.at[stream, c],
            device_id={"tensor": 1 - side}, device_id_type=MESH,
        )

    def pass_on(stream, c):
        where = far_weight.at[stream, weight_rows(group, c)]
        return pltpu.make_async_remote_copy(
            src_ref=where, dst_ref=where,
            send_sem=group_send.at[stream, c], recv_sem=group_recv.at[stream, c],
            device_id={"group": 1 - group}, device_id_type=MESH,
        )

    def relay(stream, c):
        across(stream, c).wait_recv()
        pass_on(stream, c).start()

    def load(stream):
        return pltpu.make_async_copy(
            weight.at[stream], own_weight.at[stream], load_sem.at[stream]
        )

    def hand_over(h, which):
        if which == 2:
            target = {"seq": other_core}
        else:
            target = {"tensor": 1 - side, "seq": core if which == 0 else other_core}
        return pltpu.make_async_remote_copy(
            src_ref=returned.at[h], dst_ref=full.at[side, h],
            send_sem=full_send.at[min(which, 1), h], recv_sem=full_recv.at[side, h],
            device_id=target, device_id_type=MESH,
        )

    def received(origin, h):
        where = full.at[origin, h]
        return pltpu.make_async_remote_copy(
            src_ref=where, dst_ref=where,
            send_sem=full_send.at[0, h], recv_sem=full_recv.at[origin, h],
            device_id={"seq": other_core}, device_id_type=MESH,
        )

    straight = side == core

    def distribute(h):
        @pl.when(straight)
        def _():
            hand_over(h, 2).start()
            full[side, h] = returned[h]

        @pl.when(jnp.logical_not(straight))
        def _():
            hand_over(h, 0).start()
            hand_over(h, 1).start()

    factor = hd ** (-0.5) * math.log2(math.e)

    def attend(rows_q, h):
        keys = held[h, :, 0].reshape(8 * rows, hd)
        values = held[h, :, 1].reshape(8 * rows, hd)
        values = jnp.concatenate([values, jnp.ones_like(values)], 1)
        half = rows // 2
        parts = []
        for start in (0, half):
            scores = lax.dot_general(
                rows_q[h, start : start + half],
                keys,
                (((1,), (1,)), ((), ())),
                preferred_element_type=jnp.float32,
            )
            weights = jnp.exp2(scores * factor).astype(jnp.bfloat16)
            total = jnp.dot(weights, values, preferred_element_type=jnp.float32)
            parts.append((total[:, :hd] / total[:, hd:]).astype(jnp.bfloat16))
        return jnp.concatenate(parts, 0)

    barrier = pltpu.get_barrier_semaphore()
    pl.semaphore_signal(barrier, inc=1, device_id={"seq": other_core}, device_id_type=MESH)
    pl.semaphore_signal(barrier, inc=1, device_id={"patch": inner}, device_id_type=MESH)

    for target in (
        {"group": 1 - group},
        {"tensor": 1 - side},
        {"tensor": 1 - side, "seq": other_core},
    ):
        pl.semaphore_signal(barrier, inc=1, device_id=target, device_id_type=MESH)

    @pl.when(is_mid)
    def _():
        pl.semaphore_signal(barrier, inc=1, device_id={"patch": outer}, device_id_type=MESH)

    pl.semaphore_wait(barrier, jnp.where(is_end, 5, 6))

    def arrived(h, source):
        along(h, source, inner, in_send).wait_recv()

    def siblings(h):
        def one(source, carry):
            aside(h, source).wait_recv()
            return carry

        lax.fori_loop(0, 4, one, 0)

    def store_own(h, carry):
        held[h, slot(chip)] = pair[h]
        return carry

    lax.fori_loop(0, heads, store_own, 0)

    def start_weights():
        for c in range(CHUNKS):
            across(1, c).start()

        @pl.when(gives_text)
        def _():
            for c in range(CHUNKS):
                across(0, c).start()

        load(1).start()

        @pl.when(has_text)
        def _():
            load(0).start()

    @pl.when(is_end)
    def _():
        def push(h, carry):
            along(h, chip, inner, in_send).start()

            @pl.when(h < shared)
            def _():
                aside(h, chip).start()

            @pl.when(h >= shared)
            def _():
                lend(h).start()

            return carry

        lax.fori_loop(0, heads, push, 0)
        start_weights()

        def step(h, carry):
            for source in (my_mid, far_mid, far_end):
                arrived(h, source)
                aside(h, source).start()
            siblings(h)
            returned[h] = attend(query, h)
            distribute(h)
            relay(1, h)
            return carry

        lax.fori_loop(0, shared, step, 0)

        def finish(h, carry):
            give_back(h).wait_recv()
            distribute(h)

            @pl.when(has_text)
            def _():
                relay(0, h - shared)

            return carry

        lax.fori_loop(shared, heads, finish, 0)

        def drain(h, carry):
            along(h, chip, inner, in_send).wait_send()

            @pl.when(h < shared)
            def _():
                for source in (chip, my_mid, far_mid, far_end):
                    aside(h, source).wait_send()

            @pl.when(h >= shared)
            def _():
                lend(h).wait_send()

            return carry

        lax.fori_loop(0, heads, drain, 0)

    @pl.when(is_mid)
    def _():
        def push(h, carry):
            @pl.when(h < 2)
            def _():
                along(h, chip, inner, in_send).start()

            @pl.when(h < shared)
            def _():
                along(h, chip, outer, out_send).start()

            aside(h, chip).start()
            return carry

        lax.fori_loop(0, heads, push, 0)

        def take_end(h):
            arrived(h, my_end)
            along(h, my_end, inner, in_send).start()
            aside(h, my_end).start()

        start_weights()
        take_end(0)

        def step(h, carry):
            @pl.when(h + 2 < heads)
            def _():
                along(h + 2, chip, inner, in_send).start()

            @pl.when(h + 1 < heads)
            def _():
                take_end(h + 1)

            for source in (far_mid, far_end):
                arrived(h, source)
                aside(h, source).start()

                @pl.when(h < shared)
                def _():
                    along(h, source, outer, out_send).start()

            siblings(h)

            @pl.when(h >= shared)
            def _():
                lend(h).wait_recv()
                mixed[h] = attend(guest, h)
                give_back(h).start()

            returned[h] = attend(query, h)
            distribute(h)

            @pl.when(h < CHUNKS)
            def _():
                relay(1, h)

            return carry

        lax.fori_loop(0, heads, step, 0)

        def drain(h, carry):
            along(h, chip, inner, in_send).wait_send()
            along(h, my_end, inner, in_send).wait_send()
            for source in (chip, my_end, far_mid, far_end):
                aside(h, source).wait_send()

            @pl.when(h < shared)
            def _():
                for source in (chip, far_mid, far_end):
                    along(h, source, outer, out_send).wait_send()

            @pl.when(h >= shared)
            def _():
                give_back(h).wait_send()

            return carry

        lax.fori_loop(0, heads, drain, 0)

    load(1).wait()
    for c in range(CHUNKS):
        pass_on(1, c).wait_recv()

    @pl.when(has_text)
    def _():
        load(0).wait()
        for c in range(CHUNKS):
            pass_on(0, c).wait_recv()

    def collect(h, carry):
        received(1 - side, h).wait_recv()

        @pl.when(jnp.logical_not(straight))
        def _():
            received(side, h).wait_recv()

        return carry

    lax.fori_loop(0, heads, collect, 0)
    own_rows = jnp.concatenate([full[side, h] for h in range(heads)], 1)
    far_rows = jnp.concatenate([full[1 - side, h] for h in range(heads)], 1)
    width = 512

    def project(first, last, stream, place):
        sums = jnp.dot(
            own_rows[first:last], own_weight[stream, :, place], preferred_element_type=jnp.float32
        ) + jnp.dot(
            far_rows[first:last], far_weight[stream, :, place], preferred_element_type=jnp.float32
        )
        out[first:last, place] = (sums * gates[stream : stream + 1, place]).astype(out.dtype)

    def block(index, carry):
        place = pl.ds(pl.multiple_of(index * width, width), width)

        @pl.when(has_text)
        def _():
            project(0, text_rows, 0, place)
            project(text_rows, rows, 1, place)

        @pl.when(jnp.logical_not(has_text))
        def _():
            project(0, rows, 1, place)

        return carry

    lax.fori_loop(0, columns // width, block, 0)

    def drain_rows(h, carry):
        @pl.when(straight)
        def _():
            hand_over(h, 2).wait_send()

        @pl.when(jnp.logical_not(straight))
        def _():
            hand_over(h, 0).wait_send()
            hand_over(h, 1).wait_send()

        return carry

    lax.fori_loop(0, heads, drain_rows, 0)
    for c in range(CHUNKS):
        across(1, c).wait_send()
        pass_on(1, c).wait_send()

    @pl.when(gives_text)
    def _():
        for c in range(CHUNKS):
            across(0, c).wait_send()

    @pl.when(has_text)
    def _():
        for c in range(CHUNKS):
            pass_on(0, c).wait_send()


def attend_call(query, pair, gates, weight):
    heads, rows, hd = query.shape
    dma = pltpu.SemaphoreType.DMA
    vmem = lambda *shape: pltpu.VMEM(shape, jnp.bfloat16)
    return pl.pallas_call(
        attend_kernel,
        out_shape=jax.ShapeDtypeStruct((rows, weight.shape[2]), jnp.bfloat16),
        in_specs=[pl.BlockSpec(memory_space=pltpu.VMEM)] * 3
        + [pl.BlockSpec(memory_space=pl.ANY)],
        out_specs=pl.BlockSpec(memory_space=pltpu.VMEM),
        scratch_shapes=[
            vmem(heads, 8, 2, rows, hd),
            vmem(heads, rows, hd),
            vmem(heads, rows, hd),
            vmem(heads, rows, hd),
            vmem(2, heads, rows, hd),
            vmem(*weight.shape),
            vmem(*weight.shape),
        ]
        + [dma((heads, 4))] * 5
        + [dma((heads,))] * 4
        + [dma((2, heads))] * 2
        + [dma((2, CHUNKS))] * 4
        + [dma((2,))],
        compiler_params=pltpu.CompilerParams(
            collective_id=0, has_side_effects=True, vmem_limit_bytes=60 * 2**20
        ),
    )(query, pair, gates, weight)


def on_device_line(
    query_raw,
    key_raw,
    value_raw,
    key_cache,
    value_cache,
    norm_gain,
    layout,
    group_size,
    step_index,
    gate_table,
    out_weight,
):
    query_rot, pair, key_mine, value_mine = prepare_call(
        query_raw, key_raw, value_raw, key_cache, value_cache, norm_gain, layout, group_size
    )
    chosen = (jnp.arange(gate_table.shape[1]) == step_index[0]).astype(jnp.float32)
    gates = jnp.sum(gate_table * chosen[None, :, None], 1)
    return (attend_call(query_rot, pair, gates, out_weight), key_mine, value_mine)


def solution(mesh):
    in_specs = (
        P(("group", "patch", "seq"), "tensor"),
        P(("group", "patch", "seq"), "tensor"),
        P(("group", "patch", "seq"), "tensor"),
        P(("group", "patch", "seq"), "tensor"),
        P(("group", "patch", "seq"), "tensor"),
        P(),
        P(None, ("group", "patch", "seq")),
        P("tensor"),
        P("group"),
        P(None, None, "seq"),
        P(None, "tensor", "seq"),
    )
    out_specs = (
        P(("group", "patch", "tensor"), "seq"),
        P(("group", "patch", "seq"), "tensor"),
        P(("group", "patch", "seq"), "tensor"),
    )
    fast = mesh.shape["patch"] == 4 and mesh.shape["tensor"] == 2 and mesh.shape["seq"] == 2
    return jax.shard_map(
        on_device_line if fast else on_device, mesh=mesh, in_specs=in_specs, out_specs=out_specs, check_vma=False
    )
```

```python
import functools
import math
import jax
import jax.numpy as jnp
import numpy as np
from jax import lax
from jax.experimental import pallas as pl
from jax.experimental.pallas import tpu as pltpu
from jax.sharding import PartitionSpec as P

RA = 16
RB = 56


rope_theta = 10000.0
norm_eps = 1e-06


def rope_tables(positions, plain_dims, rotary_dims):
    half_len = rotary_dims // 2
    exponent = jnp.arange(half_len, dtype=jnp.float32) * (2.0 / rotary_dims)
    freqs = jnp.exp(-jnp.log(rope_theta) * exponent)
    token_count = positions.shape[1]
    cosine = [jnp.ones((token_count, plain_dims), jnp.float32)]
    sine_part = [jnp.zeros((token_count, plain_dims), jnp.float32)]
    for which in range(2):
        angle = positions[which].astype(jnp.float32)[:, None] * freqs[None, :]
        cosine += [jnp.cos(angle), jnp.cos(angle)]
        sine_part += [jnp.sin(angle), jnp.sin(angle)]
    return (jnp.concatenate(cosine, 1), jnp.concatenate(sine_part, 1))


def partner(values, plain_dims, rotary_dims):
    half_len = rotary_dims // 2
    second = plain_dims + rotary_dims
    return jnp.concatenate(
        [
            values[..., :plain_dims],
            -values[..., plain_dims + half_len : second],
            values[..., plain_dims : plain_dims + half_len],
            -values[..., second + half_len :],
            values[..., second : second + half_len],
        ],
        -1,
    )


def compress(residual, group_size, heads, head_dim):
    row_count = residual.shape[0]
    halves = residual.reshape(row_count, heads, 2, head_dim // 2)
    half_ms = jnp.mean(halves * halves, -1)
    whole_ms = jnp.mean(half_ms, -1, keepdims=True)
    whole = (group_size == head_dim)[None, :, None]
    mean_sq = jnp.where(whole, whole_ms, half_ms)
    scales = jnp.sqrt(mean_sq + norm_eps).astype(jnp.bfloat16)
    codes = jnp.tanh(halves / scales.astype(jnp.float32)[..., None]).astype(jnp.bfloat16)
    return (codes.reshape(row_count, heads * head_dim), scales.reshape(row_count, heads * 2))


def decode(codes, scales, heads, head_dim):
    row_count = codes.shape[0]
    parts = codes.astype(jnp.float32).reshape(row_count, heads, 2, head_dim // 2) * scales.astype(
        jnp.float32
    ).reshape(row_count, heads, 2, 1)
    return parts.reshape(row_count, heads * head_dim)


def prepare(query_raw, key_raw, value_raw, positions, norm_gain, key_rows, value_rows, group_size):
    row_count = query_raw.shape[0]
    heads = group_size.shape[0]
    head_dim = norm_gain.shape[-1]
    text_rows = (positions[0] == 0)[:, None, None]
    cosine, sine_part = rope_tables(positions, RA, RB)
    cosine = cosine[:, None, :]
    sine_part = sine_part[:, None, :]

    def embed(raw, which):
        gain = jnp.where(
            text_rows, norm_gain[0, which][None, None, :], norm_gain[1, which][None, None, :]
        )
        values = raw.astype(jnp.float32).reshape(row_count, heads, head_dim)
        normed = values * lax.rsqrt(jnp.mean(values * values, -1, keepdims=True) + norm_eps) * gain
        return (normed * cosine + partner(normed, RA, RB) * sine_part).reshape(
            row_count, heads * head_dim
        )

    query_rot = embed(query_raw, 0).astype(jnp.bfloat16)
    key_rot = embed(key_raw, 1)
    key_codes, key_scales = compress(
        key_rot - key_rows.astype(jnp.float32), group_size, heads, head_dim
    )
    value_codes, value_scales = compress(
        value_raw.astype(jnp.float32) - value_rows.astype(jnp.float32), group_size, heads, head_dim
    )
    return (query_rot, key_codes, value_codes, key_scales, value_scales)


def block_length(piece_rows):
    for candidate in range(min(piece_rows, 2048), 0, -1):
        if piece_rows % candidate == 0:
            return candidate
    return piece_rows


def on_device(
    query_raw,
    key_raw,
    value_raw,
    key_cache,
    value_cache,
    norm_gain,
    layout,
    group_size,
    step_index,
    gate_table,
    out_weight,
):
    row_count = query_raw.shape[0]
    heads = group_size.shape[0]
    head_dim = norm_gain.shape[-1]
    query_rot, key_codes, value_codes, key_scales, value_scales = prepare(
        query_raw, key_raw, value_raw, layout, norm_gain, key_cache, value_cache, group_size
    )
    key_mine = (
        key_cache.astype(jnp.float32) + decode(key_codes, key_scales, heads, head_dim)
    ).astype(jnp.bfloat16)
    value_mine = (
        value_cache.astype(jnp.float32) + decode(value_codes, value_scales, heads, head_dim)
    ).astype(jnp.bfloat16)
    query_heads = query_rot.reshape(row_count, heads, head_dim)
    inverse_root = head_dim ** (-0.5)
    start_state = (
        jnp.zeros((heads, row_count, head_dim), jnp.float32),
        jnp.zeros((heads, row_count), jnp.float32),
    )
    keys_all = lax.all_gather(key_mine, ("patch", "seq"), axis=0, tiled=True)
    values_all = lax.all_gather(value_mine, ("patch", "seq"), axis=0, tiled=True)
    piece_rows = keys_all.shape[0]
    length = block_length(piece_rows)

    def one_block(index, carry):
        numer, totals = carry
        keys = lax.dynamic_slice_in_dim(keys_all, index * length, length, 0).reshape(
            length, heads, head_dim
        )
        values = lax.dynamic_slice_in_dim(values_all, index * length, length, 0).reshape(
            length, heads, head_dim
        )
        scores = (
            jnp.einsum("qhd,khd->hqk", query_heads, keys, preferred_element_type=jnp.float32)
            * inverse_root
        )
        weights = jnp.exp(scores)
        totals = totals + jnp.sum(weights, -1)
        numer = numer + jnp.einsum(
            "hqk,khd->hqd", weights.astype(jnp.bfloat16), values, preferred_element_type=jnp.float32
        )
        return (numer, totals)

    numer, totals = lax.fori_loop(0, piece_rows // length, one_block, start_state)
    attn_rows = (
        (numer / totals[..., None])
        .transpose(1, 0, 2)
        .reshape(row_count, heads * head_dim)
        .astype(jnp.bfloat16)
    )
    text_flag = (layout[0] == 0).astype(jnp.bfloat16)
    pair_attn, pair_text = (
        lax.all_gather(attn_rows, "seq", axis=0, tiled=True),
        lax.all_gather(text_flag, "seq", axis=0, tiled=True),
    )
    share = pair_attn.shape[0] // lax.axis_size("tensor")

    def both_streams(block, block_text):
        text_part = jnp.dot(block, out_weight[0], preferred_element_type=jnp.float32)
        image_part = jnp.dot(block, out_weight[1], preferred_element_type=jnp.float32)
        return jnp.where(block_text[:, None] > 0, text_part, image_part)

    def image_only(block, block_text):
        return jnp.dot(block, out_weight[1], preferred_element_type=jnp.float32)

    block = pair_attn
    block_text = pair_text
    projected = lax.psum_scatter(
        lax.cond(jnp.any(block_text > 0), both_streams, image_only, block, block_text),
        "tensor",
        scatter_dimension=0,
        tiled=True,
    )
    mine_text = lax.dynamic_slice_in_dim(pair_text, lax.axis_index("tensor") * share, share, 0)
    chosen = (jnp.arange(gate_table.shape[1]) == step_index[0]).astype(jnp.float32)
    gates = jnp.sum(gate_table * chosen[None, :, None], 1)
    gate_rows = jnp.where(mine_text[:, None] > 0, gates[0][None, :], gates[1][None, :])
    return ((gate_rows * projected).astype(jnp.bfloat16), key_mine, value_mine)


MESH = pl.DeviceIdType.MESH
GATHER_SHARE = 2
CHUNKS = 6
TEXT_PART = 12


def lane_tables(head_dim):
    half_len = RB // 2
    freqs = np.exp(-math.log(rope_theta) * np.arange(half_len) * (2.0 / RB)).astype(np.float32)
    table = np.zeros((8, head_dim), np.float32)
    for which in range(2):
        start = RA + which * RB
        table[which, start : start + half_len] = freqs
        table[which, start + half_len : start + RB] = freqs
        table[2, start : start + half_len] = -1.0
        table[3, start + half_len : start + RB] = 1.0
    return jnp.asarray(table)


def split_dot(values, matrix):
    high = values.astype(jnp.bfloat16)
    low = (values - high.astype(jnp.float32)).astype(jnp.bfloat16)
    return jnp.dot(
        jnp.concatenate([high, low], 1),
        jnp.concatenate([matrix, matrix], 0),
        preferred_element_type=jnp.float32,
    )


def prepare_kernel(
    sizes, positions, gains, table, query, key, value, key_old, value_old,
    query_out, pair_out, key_out, value_out, cosine, sine_low, sine_high, gain_q, gain_k,
):
    head = pl.program_id(0)
    head_dim = query.shape[1]
    half_len = RB // 2

    @pl.when(head == 0)
    def _():
        rows_id = positions[:, 0:1]
        angle = rows_id * table[0:1, :] + positions[:, 1:2] * table[1:2, :]
        sine = jnp.sin(angle)
        cosine[...] = jnp.cos(angle)
        sine_low[...] = sine * table[2:3, :]
        sine_high[...] = sine * table[3:4, :]
        text = rows_id == 0
        gain_q[...] = jnp.where(text, gains[0:1, :], gains[2:3, :])
        gain_k[...] = jnp.where(text, gains[1:2, :], gains[3:4, :])

    full = jnp.full((head_dim, head_dim), 1.0 / head_dim, jnp.float32)
    row = lax.broadcasted_iota(jnp.int32, (head_dim, head_dim), 0) < head_dim // 2
    col = lax.broadcasted_iota(jnp.int32, (head_dim, head_dim), 1) < head_dim // 2
    halves = jnp.where(row == col, 2.0 / head_dim, 0.0)
    whole = (sizes[head] == head_dim).astype(jnp.float32)
    grouped = (whole * full + (1.0 - whole) * halves).astype(jnp.bfloat16)
    full = full.astype(jnp.bfloat16)

    def embed(raw, gain):
        values = raw[...].astype(jnp.float32)
        normed = values * lax.rsqrt(split_dot(values * values, full) + norm_eps) * gain[...]
        return (
            normed * cosine[...]
            + pltpu.roll(normed, head_dim - half_len, 1) * sine_low[...]
            + pltpu.roll(normed, half_len, 1) * sine_high[...]
        )

    def update(fresh, old):
        kept = old[...].astype(jnp.float32)
        residual = fresh - kept
        scale = jnp.sqrt(split_dot(residual * residual, grouped) + norm_eps)
        scale = scale.astype(jnp.bfloat16).astype(jnp.float32)
        code = jnp.tanh(residual / scale).astype(jnp.bfloat16).astype(jnp.float32)
        return (kept + scale * code).astype(jnp.bfloat16)

    query_out[0] = embed(query, gain_q).astype(jnp.bfloat16)
    key_next = update(embed(key, gain_k), key_old)
    value_next = update(value[...].astype(jnp.float32), value_old)
    pair_out[0, 0] = key_next
    pair_out[0, 1] = value_next
    key_out[...] = key_next
    value_out[...] = value_next


def prepare_call(query, key, value, key_old, value_old, norm_gain, layout, group_size):
    rows, width = query.shape
    heads = group_size.shape[0]
    hd = width // heads
    block = pl.BlockSpec((rows, hd), lambda h: (0, h))
    whole = lambda *shape: pl.BlockSpec(shape, lambda h: (0,) * len(shape))
    return pl.pallas_call(
        prepare_kernel,
        grid=(heads,),
        in_specs=[
            pl.BlockSpec(memory_space=pltpu.SMEM),
            whole(rows, 2),
            whole(4, hd),
            whole(8, hd),
        ]
        + [block] * 5,
        out_specs=[
            pl.BlockSpec((1, rows, hd), lambda h: (h, 0, 0)),
            pl.BlockSpec((1, 2, rows, hd), lambda h: (h, 0, 0, 0)),
            block,
            block,
        ],
        out_shape=[
            jax.ShapeDtypeStruct((heads, rows, hd), jnp.bfloat16),
            jax.ShapeDtypeStruct((heads, 2, rows, hd), jnp.bfloat16),
            jax.ShapeDtypeStruct((rows, width), jnp.bfloat16),
            jax.ShapeDtypeStruct((rows, width), jnp.bfloat16),
        ],
        scratch_shapes=[pltpu.VMEM((rows, hd), jnp.float32)] * 5,
        compiler_params=pltpu.CompilerParams(vmem_limit_bytes=60 * 2**20),
    )(
        group_size,
        layout.astype(jnp.float32).T,
        norm_gain.reshape(4, hd),
        lane_tables(hd),
        query,
        key,
        value,
        key_old,
        value_old,
    )


def attend_kernel(
    query, pair, gates, weight, out, held, guest, mixed, returned, full, own_weight, far_weight,
    in_send, out_send, side_send, line_recv, side_recv, guest_send, guest_recv, back_send,
    back_recv, full_send, full_recv, across_send, across_recv, group_send, group_recv, load_sem,
):
    heads, rows, hd = query.shape
    features, columns = weight.shape[1:]
    group = lax.axis_index("group")
    side = lax.axis_index("tensor")
    shared = heads // GATHER_SHARE
    chip = lax.axis_index("patch")
    core = lax.axis_index("seq")
    other_core = 1 - core
    upper = chip // 2
    is_end = (chip == 0) | (chip == 3)
    is_mid = jnp.logical_not(is_end)
    my_end = upper * 3
    my_mid = 1 + upper
    far_mid = 2 - upper
    far_end = 3 - my_end
    inner = jnp.where(is_end, my_mid, far_mid)
    outer = my_end

    def slot(source):
        return source * 2 + core

    def to_chip(src, dst, send, recv, target):
        return pltpu.make_async_remote_copy(
            src_ref=src, dst_ref=dst, send_sem=send, recv_sem=recv,
            device_id={"patch": target}, device_id_type=MESH,
        )

    def along(h, source, target, send):
        where = held.at[h, slot(source)]
        return to_chip(where, where, send.at[h, source], line_recv.at[h, source], target)

    def aside(h, source):
        where = held.at[h, slot(source)]
        return pltpu.make_async_remote_copy(
            src_ref=where, dst_ref=where, send_sem=side_send.at[h, source],
            recv_sem=side_recv.at[h, source],
            device_id={"seq": other_core}, device_id_type=MESH,
        )

    def lend(h):
        return to_chip(
            query.at[h], guest.at[h], guest_send.at[h], guest_recv.at[h], inner
        )

    def give_back(h):
        return to_chip(
            mixed.at[h], returned.at[h], back_send.at[h], back_recv.at[h], outer
        )

    has_text = (chip == 0) & (side == 0)
    gives_text = (chip == 0) & (side == 1)
    text_rows = rows * 8 // TEXT_PART
    chunk = features // 2 // CHUNKS

    def weight_rows(owner, c):
        return pl.ds(pl.multiple_of(owner * (features // 2) + c * chunk, chunk), chunk)

    def across(stream, c):
        where = weight_rows(group, c)
        return pltpu.make_async_remote_copy(
            src_ref=weight.at[stream, where], dst_ref=far_weight.at[stream, where],
            send_sem=across_send.at[stream, c], recv_sem=across_recv.at[stream, c],
            device_id={"tensor": 1 - side}, device_id_type=MESH,
        )

    def pass_on(stream, c):
        where = far_weight.at[stream, weight_rows(group, c)]
        return pltpu.make_async_remote_copy(
            src_ref=where, dst_ref=where,
            send_sem=group_send.at[stream, c], recv_sem=group_recv.at[stream, c],
            device_id={"group": 1 - group}, device_id_type=MESH,
        )

    def relay(stream, c):
        across(stream, c).wait_recv()
        pass_on(stream, c).start()

    def load(stream):
        return pltpu.make_async_copy(
            weight.at[stream], own_weight.at[stream], load_sem.at[stream]
        )

    def hand_over(h, which):
        if which == 2:
            target = {"seq": other_core}
        else:
            target = {"tensor": 1 - side, "seq": core if which == 0 else other_core}
        return pltpu.make_async_remote_copy(
            src_ref=returned.at[h], dst_ref=full.at[side, h],
            send_sem=full_send.at[min(which, 1), h], recv_sem=full_recv.at[side, h],
            device_id=target, device_id_type=MESH,
        )

    def received(origin, h):
        where = full.at[origin, h]
        return pltpu.make_async_remote_copy(
            src_ref=where, dst_ref=where,
            send_sem=full_send.at[0, h], recv_sem=full_recv.at[origin, h],
            device_id={"seq": other_core}, device_id_type=MESH,
        )

    straight = side == core

    def distribute(h):
        @pl.when(straight)
        def _():
            hand_over(h, 2).start()
            full[side, h] = returned[h]

        @pl.when(jnp.logical_not(straight))
        def _():
            hand_over(h, 0).start()
            hand_over(h, 1).start()

    factor = hd ** (-0.5) * math.log2(math.e)

    def attend(rows_q, h):
        keys = held[h, :, 0].reshape(8 * rows, hd)
        values = held[h, :, 1].reshape(8 * rows, hd)
        values = jnp.concatenate([values, jnp.ones_like(values)], 1)
        half = rows // 2
        parts = []
        for start in (0, half):
            scores = lax.dot_general(
                rows_q[h, start : start + half],
                keys,
                (((1,), (1,)), ((), ())),
                preferred_element_type=jnp.float32,
            )
            weights = jnp.exp2(scores * factor).astype(jnp.bfloat16)
            total = jnp.dot(weights, values, preferred_element_type=jnp.float32)
            parts.append((total[:, :hd] / total[:, hd:]).astype(jnp.bfloat16))
        return jnp.concatenate(parts, 0)

    barrier = pltpu.get_barrier_semaphore()
    pl.semaphore_signal(barrier, inc=1, device_id={"seq": other_core}, device_id_type=MESH)
    pl.semaphore_signal(barrier, inc=1, device_id={"patch": inner}, device_id_type=MESH)

    for target in (
        {"group": 1 - group},
        {"tensor": 1 - side},
        {"tensor": 1 - side, "seq": other_core},
    ):
        pl.semaphore_signal(barrier, inc=1, device_id=target, device_id_type=MESH)

    @pl.when(is_mid)
    def _():
        pl.semaphore_signal(barrier, inc=1, device_id={"patch": outer}, device_id_type=MESH)

    pl.semaphore_wait(barrier, jnp.where(is_end, 5, 6))

    def arrived(h, source):
        along(h, source, inner, in_send).wait_recv()

    def siblings(h):
        def one(source, carry):
            aside(h, source).wait_recv()
            return carry

        lax.fori_loop(0, 4, one, 0)

    def start_weights():
        @pl.when(gives_text)
        def _():
            for c in range(CHUNKS):
                across(0, c).start()

        for c in range(CHUNKS):
            across(1, c).start()

        load(1).start()

        @pl.when(has_text)
        def _():
            load(0).start()

    @pl.when(is_end)
    def _():
        def push(h, carry):
            held[h, slot(chip)] = pair[h]
            along(h, chip, inner, in_send).start()

            @pl.when(h < shared)
            def _():
                aside(h, chip).start()

            @pl.when(h >= shared)
            def _():
                lend(h).start()

            return carry

        lax.fori_loop(0, heads, push, 0)
        start_weights()

        def step(h, carry):
            for source in (my_mid, far_mid, far_end):
                arrived(h, source)
                aside(h, source).start()
            siblings(h)
            returned[h] = attend(query, h)
            distribute(h)

            @pl.when(has_text)
            def _():
                for c in range(2):
                    relay(0, 2 * h + c)

            return carry

        lax.fori_loop(0, shared, step, 0)

        def finish(h, carry):
            for c in range(2):
                relay(1, 2 * (h - shared) + c)
            give_back(h).wait_recv()
            distribute(h)
            return carry

        lax.fori_loop(shared, heads, finish, 0)

        def drain(h, carry):
            along(h, chip, inner, in_send).wait_send()

            @pl.when(h < shared)
            def _():
                for source in (chip, my_mid, far_mid, far_end):
                    aside(h, source).wait_send()

            @pl.when(h >= shared)
            def _():
                lend(h).wait_send()

            return carry

        lax.fori_loop(0, heads, drain, 0)

    @pl.when(is_mid)
    def _():
        def push(h, carry):
            held[h, slot(chip)] = pair[h]
            @pl.when(h < 2)
            def _():
                along(h, chip, inner, in_send).start()

            @pl.when(h < shared)
            def _():
                along(h, chip, outer, out_send).start()

            aside(h, chip).start()
            return carry

        lax.fori_loop(0, heads, push, 0)

        def take_end(h):
            arrived(h, my_end)
            along(h, my_end, inner, in_send).start()
            aside(h, my_end).start()

        start_weights()
        take_end(0)

        def step(h, carry):
            @pl.when(h + 2 < heads)
            def _():
                along(h + 2, chip, inner, in_send).start()

            @pl.when(h + 1 < heads)
            def _():
                take_end(h + 1)

            for source in (far_mid, far_end):
                arrived(h, source)
                aside(h, source).start()

                @pl.when(h < shared)
                def _():
                    along(h, source, outer, out_send).start()

            siblings(h)

            @pl.when(h >= shared)
            def _():
                lend(h).wait_recv()
                mixed[h] = attend(guest, h)
                give_back(h).start()

            returned[h] = attend(query, h)
            distribute(h)

            relay(1, h)
            return carry

        lax.fori_loop(0, heads, step, 0)

        def drain(h, carry):
            along(h, chip, inner, in_send).wait_send()
            along(h, my_end, inner, in_send).wait_send()
            for source in (chip, my_end, far_mid, far_end):
                aside(h, source).wait_send()

            @pl.when(h < shared)
            def _():
                for source in (chip, far_mid, far_end):
                    along(h, source, outer, out_send).wait_send()

            @pl.when(h >= shared)
            def _():
                give_back(h).wait_send()

            return carry

        lax.fori_loop(0, heads, drain, 0)

    load(1).wait()
    for c in range(CHUNKS):
        pass_on(1, c).wait_recv()

    @pl.when(has_text)
    def _():
        load(0).wait()
        for c in range(CHUNKS):
            pass_on(0, c).wait_recv()

    def collect(h, carry):
        received(1 - side, h).wait_recv()

        @pl.when(jnp.logical_not(straight))
        def _():
            received(side, h).wait_recv()

        return carry

    lax.fori_loop(0, heads, collect, 0)
    own_rows = jnp.concatenate([full[side, h] for h in range(heads)], 1)
    far_rows = jnp.concatenate([full[1 - side, h] for h in range(heads)], 1)
    width = 512

    def project(first, last, stream, place):
        sums = jnp.dot(
            own_rows[first:last], own_weight[stream, :, place], preferred_element_type=jnp.float32
        ) + jnp.dot(
            far_rows[first:last], far_weight[stream, :, place], preferred_element_type=jnp.float32
        )
        out[first:last, place] = (sums * gates[stream : stream + 1, place]).astype(out.dtype)

    def block(index, carry):
        place = pl.ds(pl.multiple_of(index * width, width), width)

        @pl.when(has_text)
        def _():
            project(0, text_rows, 0, place)
            project(text_rows, rows, 1, place)

        @pl.when(jnp.logical_not(has_text))
        def _():
            project(0, rows, 1, place)

        return carry

    lax.fori_loop(0, columns // width, block, 0)

    def drain_rows(h, carry):
        @pl.when(straight)
        def _():
            hand_over(h, 2).wait_send()

        @pl.when(jnp.logical_not(straight))
        def _():
            hand_over(h, 0).wait_send()
            hand_over(h, 1).wait_send()

        return carry

    lax.fori_loop(0, heads, drain_rows, 0)
    for c in range(CHUNKS):
        across(1, c).wait_send()
        pass_on(1, c).wait_send()

    @pl.when(gives_text)
    def _():
        for c in range(CHUNKS):
            across(0, c).wait_send()

    @pl.when(has_text)
    def _():
        for c in range(CHUNKS):
            pass_on(0, c).wait_send()


def attend_call(query, pair, gates, weight):
    heads, rows, hd = query.shape
    dma = pltpu.SemaphoreType.DMA
    vmem = lambda *shape: pltpu.VMEM(shape, jnp.bfloat16)
    return pl.pallas_call(
        attend_kernel,
        out_shape=jax.ShapeDtypeStruct((rows, weight.shape[2]), jnp.bfloat16),
        in_specs=[pl.BlockSpec(memory_space=pltpu.VMEM)] * 3
        + [pl.BlockSpec(memory_space=pl.ANY)],
        out_specs=pl.BlockSpec(memory_space=pltpu.VMEM),
        scratch_shapes=[
            vmem(heads, 8, 2, rows, hd),
            vmem(heads, rows, hd),
            vmem(heads, rows, hd),
            vmem(heads, rows, hd),
            vmem(2, heads, rows, hd),
            vmem(*weight.shape),
            vmem(*weight.shape),
        ]
        + [dma((heads, 4))] * 5
        + [dma((heads,))] * 4
        + [dma((2, heads))] * 2
        + [dma((2, CHUNKS))] * 4
        + [dma((2,))],
        compiler_params=pltpu.CompilerParams(
            collective_id=0, has_side_effects=True, vmem_limit_bytes=60 * 2**20
        ),
    )(query, pair, gates, weight)


def on_device_line(
    query_raw,
    key_raw,
    value_raw,
    key_cache,
    value_cache,
    norm_gain,
    layout,
    group_size,
    step_index,
    gate_table,
    out_weight,
):
    query_rot, pair, key_mine, value_mine = prepare_call(
        query_raw, key_raw, value_raw, key_cache, value_cache, norm_gain, layout, group_size
    )
    chosen = (jnp.arange(gate_table.shape[1]) == step_index[0]).astype(jnp.float32)
    gates = jnp.sum(gate_table * chosen[None, :, None], 1)
    return (attend_call(query_rot, pair, gates, out_weight), key_mine, value_mine)


def solution(mesh):
    in_specs = (
        P(("group", "patch", "seq"), "tensor"),
        P(("group", "patch", "seq"), "tensor"),
        P(("group", "patch", "seq"), "tensor"),
        P(("group", "patch", "seq"), "tensor"),
        P(("group", "patch", "seq"), "tensor"),
        P(),
        P(None, ("group", "patch", "seq")),
        P("tensor"),
        P("group"),
        P(None, None, "seq"),
        P(None, "tensor", "seq"),
    )
    out_specs = (
        P(("group", "patch", "tensor"), "seq"),
        P(("group", "patch", "seq"), "tensor"),
        P(("group", "patch", "seq"), "tensor"),
    )
    fast = mesh.shape["patch"] == 4 and mesh.shape["tensor"] == 2 and mesh.shape["seq"] == 2
    return jax.shard_map(
        on_device_line if fast else on_device, mesh=mesh, in_specs=in_specs, out_specs=out_specs, check_vma=False
    )
```

```python
import functools
import math
import jax
import jax.numpy as jnp
import numpy as np
from jax import lax
from jax.experimental import pallas as pl
from jax.experimental.pallas import tpu as pltpu
from jax.sharding import PartitionSpec as P

RA = 16
RB = 56


rope_theta = 10000.0
norm_eps = 1e-06


def rope_tables(positions, plain_dims, rotary_dims):
    half_len = rotary_dims // 2
    exponent = jnp.arange(half_len, dtype=jnp.float32) * (2.0 / rotary_dims)
    freqs = jnp.exp(-jnp.log(rope_theta) * exponent)
    token_count = positions.shape[1]
    cosine = [jnp.ones((token_count, plain_dims), jnp.float32)]
    sine_part = [jnp.zeros((token_count, plain_dims), jnp.float32)]
    for which in range(2):
        angle = positions[which].astype(jnp.float32)[:, None] * freqs[None, :]
        cosine += [jnp.cos(angle), jnp.cos(angle)]
        sine_part += [jnp.sin(angle), jnp.sin(angle)]
    return (jnp.concatenate(cosine, 1), jnp.concatenate(sine_part, 1))


def partner(values, plain_dims, rotary_dims):
    half_len = rotary_dims // 2
    second = plain_dims + rotary_dims
    return jnp.concatenate(
        [
            values[..., :plain_dims],
            -values[..., plain_dims + half_len : second],
            values[..., plain_dims : plain_dims + half_len],
            -values[..., second + half_len :],
            values[..., second : second + half_len],
        ],
        -1,
    )


def compress(residual, group_size, heads, head_dim):
    row_count = residual.shape[0]
    halves = residual.reshape(row_count, heads, 2, head_dim // 2)
    half_ms = jnp.mean(halves * halves, -1)
    whole_ms = jnp.mean(half_ms, -1, keepdims=True)
    whole = (group_size == head_dim)[None, :, None]
    mean_sq = jnp.where(whole, whole_ms, half_ms)
    scales = jnp.sqrt(mean_sq + norm_eps).astype(jnp.bfloat16)
    codes = jnp.tanh(halves / scales.astype(jnp.float32)[..., None]).astype(jnp.bfloat16)
    return (codes.reshape(row_count, heads * head_dim), scales.reshape(row_count, heads * 2))


def decode(codes, scales, heads, head_dim):
    row_count = codes.shape[0]
    parts = codes.astype(jnp.float32).reshape(row_count, heads, 2, head_dim // 2) * scales.astype(
        jnp.float32
    ).reshape(row_count, heads, 2, 1)
    return parts.reshape(row_count, heads * head_dim)


def prepare(query_raw, key_raw, value_raw, positions, norm_gain, key_rows, value_rows, group_size):
    row_count = query_raw.shape[0]
    heads = group_size.shape[0]
    head_dim = norm_gain.shape[-1]
    text_rows = (positions[0] == 0)[:, None, None]
    cosine, sine_part = rope_tables(positions, RA, RB)
    cosine = cosine[:, None, :]
    sine_part = sine_part[:, None, :]

    def embed(raw, which):
        gain = jnp.where(
            text_rows, norm_gain[0, which][None, None, :], norm_gain[1, which][None, None, :]
        )
        values = raw.astype(jnp.float32).reshape(row_count, heads, head_dim)
        normed = values * lax.rsqrt(jnp.mean(values * values, -1, keepdims=True) + norm_eps) * gain
        return (normed * cosine + partner(normed, RA, RB) * sine_part).reshape(
            row_count, heads * head_dim
        )

    query_rot = embed(query_raw, 0).astype(jnp.bfloat16)
    key_rot = embed(key_raw, 1)
    key_codes, key_scales = compress(
        key_rot - key_rows.astype(jnp.float32), group_size, heads, head_dim
    )
    value_codes, value_scales = compress(
        value_raw.astype(jnp.float32) - value_rows.astype(jnp.float32), group_size, heads, head_dim
    )
    return (query_rot, key_codes, value_codes, key_scales, value_scales)


def block_length(piece_rows):
    for candidate in range(min(piece_rows, 2048), 0, -1):
        if piece_rows % candidate == 0:
            return candidate
    return piece_rows


def on_device(
    query_raw,
    key_raw,
    value_raw,
    key_cache,
    value_cache,
    norm_gain,
    layout,
    group_size,
    step_index,
    gate_table,
    out_weight,
):
    row_count = query_raw.shape[0]
    heads = group_size.shape[0]
    head_dim = norm_gain.shape[-1]
    query_rot, key_codes, value_codes, key_scales, value_scales = prepare(
        query_raw, key_raw, value_raw, layout, norm_gain, key_cache, value_cache, group_size
    )
    key_mine = (
        key_cache.astype(jnp.float32) + decode(key_codes, key_scales, heads, head_dim)
    ).astype(jnp.bfloat16)
    value_mine = (
        value_cache.astype(jnp.float32) + decode(value_codes, value_scales, heads, head_dim)
    ).astype(jnp.bfloat16)
    query_heads = query_rot.reshape(row_count, heads, head_dim)
    inverse_root = head_dim ** (-0.5)
    start_state = (
        jnp.zeros((heads, row_count, head_dim), jnp.float32),
        jnp.zeros((heads, row_count), jnp.float32),
    )
    keys_all = lax.all_gather(key_mine, ("patch", "seq"), axis=0, tiled=True)
    values_all = lax.all_gather(value_mine, ("patch", "seq"), axis=0, tiled=True)
    piece_rows = keys_all.shape[0]
    length = block_length(piece_rows)

    def one_block(index, carry):
        numer, totals = carry
        keys = lax.dynamic_slice_in_dim(keys_all, index * length, length, 0).reshape(
            length, heads, head_dim
        )
        values = lax.dynamic_slice_in_dim(values_all, index * length, length, 0).reshape(
            length, heads, head_dim
        )
        scores = (
            jnp.einsum("qhd,khd->hqk", query_heads, keys, preferred_element_type=jnp.float32)
            * inverse_root
        )
        weights = jnp.exp(scores)
        totals = totals + jnp.sum(weights, -1)
        numer = numer + jnp.einsum(
            "hqk,khd->hqd", weights.astype(jnp.bfloat16), values, preferred_element_type=jnp.float32
        )
        return (numer, totals)

    numer, totals = lax.fori_loop(0, piece_rows // length, one_block, start_state)
    attn_rows = (
        (numer / totals[..., None])
        .transpose(1, 0, 2)
        .reshape(row_count, heads * head_dim)
        .astype(jnp.bfloat16)
    )
    text_flag = (layout[0] == 0).astype(jnp.bfloat16)
    pair_attn, pair_text = (
        lax.all_gather(attn_rows, "seq", axis=0, tiled=True),
        lax.all_gather(text_flag, "seq", axis=0, tiled=True),
    )
    share = pair_attn.shape[0] // lax.axis_size("tensor")

    def both_streams(block, block_text):
        text_part = jnp.dot(block, out_weight[0], preferred_element_type=jnp.float32)
        image_part = jnp.dot(block, out_weight[1], preferred_element_type=jnp.float32)
        return jnp.where(block_text[:, None] > 0, text_part, image_part)

    def image_only(block, block_text):
        return jnp.dot(block, out_weight[1], preferred_element_type=jnp.float32)

    block = pair_attn
    block_text = pair_text
    projected = lax.psum_scatter(
        lax.cond(jnp.any(block_text > 0), both_streams, image_only, block, block_text),
        "tensor",
        scatter_dimension=0,
        tiled=True,
    )
    mine_text = lax.dynamic_slice_in_dim(pair_text, lax.axis_index("tensor") * share, share, 0)
    chosen = (jnp.arange(gate_table.shape[1]) == step_index[0]).astype(jnp.float32)
    gates = jnp.sum(gate_table * chosen[None, :, None], 1)
    gate_rows = jnp.where(mine_text[:, None] > 0, gates[0][None, :], gates[1][None, :])
    return ((gate_rows * projected).astype(jnp.bfloat16), key_mine, value_mine)


MESH = pl.DeviceIdType.MESH
GATHER_SHARE = 2
CHUNKS = 3
TEXT_PART = 12


def lane_tables(head_dim):
    half_len = RB // 2
    freqs = np.exp(-math.log(rope_theta) * np.arange(half_len) * (2.0 / RB)).astype(np.float32)
    table = np.zeros((8, head_dim), np.float32)
    for which in range(2):
        start = RA + which * RB
        table[which, start : start + half_len] = freqs
        table[which, start + half_len : start + RB] = freqs
        table[2, start : start + half_len] = -1.0
        table[3, start + half_len : start + RB] = 1.0
    return jnp.asarray(table)


def split_dot(values, matrix):
    high = values.astype(jnp.bfloat16)
    low = (values - high.astype(jnp.float32)).astype(jnp.bfloat16)
    return jnp.dot(
        jnp.concatenate([high, low], 1),
        jnp.concatenate([matrix, matrix], 0),
        preferred_element_type=jnp.float32,
    )


def attend_kernel(
    sizes, step_index, positions, gains, table, query_raw, key_raw, value_raw, key_old, value_old,
    gate_table, weight, out, key_out, value_out, query, gates, cosine, sine_low, sine_high,
    gain_q, gain_k, held, guest, mixed, returned, full, own_weight, far_weight,
    in_send, out_send, side_send, line_recv, side_recv, guest_send, guest_recv, back_send,
    back_recv, full_send, full_recv, across_send, across_recv, group_send, group_recv, load_sem,
):
    heads, rows, hd = query.shape
    features, columns = weight.shape[1:]
    group = lax.axis_index("group")
    side = lax.axis_index("tensor")
    shared = heads // GATHER_SHARE
    chip = lax.axis_index("patch")
    core = lax.axis_index("seq")
    other_core = 1 - core
    upper = chip // 2
    is_end = (chip == 0) | (chip == 3)
    is_mid = jnp.logical_not(is_end)
    my_end = upper * 3
    my_mid = 1 + upper
    far_mid = 2 - upper
    far_end = 3 - my_end
    inner = jnp.where(is_end, my_mid, far_mid)
    outer = my_end

    def slot(source):
        return source * 2 + core

    def to_chip(src, dst, send, recv, target):
        return pltpu.make_async_remote_copy(
            src_ref=src, dst_ref=dst, send_sem=send, recv_sem=recv,
            device_id={"patch": target}, device_id_type=MESH,
        )

    def along(h, source, target, send):
        where = held.at[h, slot(source)]
        return to_chip(where, where, send.at[h, source], line_recv.at[h, source], target)

    def aside(h, source):
        where = held.at[h, slot(source)]
        return pltpu.make_async_remote_copy(
            src_ref=where, dst_ref=where, send_sem=side_send.at[h, source],
            recv_sem=side_recv.at[h, source],
            device_id={"seq": other_core}, device_id_type=MESH,
        )

    def lend(h):
        return to_chip(
            query.at[h], guest.at[h], guest_send.at[h], guest_recv.at[h], inner
        )

    def give_back(h):
        return to_chip(
            mixed.at[h], returned.at[h], back_send.at[h], back_recv.at[h], outer
        )

    has_text = (chip == 0) & (side == 0)
    gives_text = (chip == 0) & (side == 1)
    text_rows = rows * 8 // TEXT_PART
    chunk = features // 2 // CHUNKS

    def weight_rows(owner, c):
        return pl.ds(pl.multiple_of(owner * (features // 2) + c * chunk, chunk), chunk)

    def across(stream, c):
        where = weight_rows(group, c)
        return pltpu.make_async_remote_copy(
            src_ref=weight.at[stream, where], dst_ref=far_weight.at[stream, where],
            send_sem=across_send.at[stream, c], recv_sem=across_recv.at[stream, c],
            device_id={"tensor": 1 - side}, device_id_type=MESH,
        )

    def pass_on(stream, c):
        where = far_weight.at[stream, weight_rows(group, c)]
        return pltpu.make_async_remote_copy(
            src_ref=where, dst_ref=where,
            send_sem=group_send.at[stream, c], recv_sem=group_recv.at[stream, c],
            device_id={"group": 1 - group}, device_id_type=MESH,
        )

    def relay(stream, c):
        across(stream, c).wait_recv()
        pass_on(stream, c).start()

    def load(stream):
        return pltpu.make_async_copy(
            weight.at[stream], own_weight.at[stream], load_sem.at[stream]
        )

    def hand_over(h, which):
        if which == 2:
            target = {"seq": other_core}
        else:
            target = {"tensor": 1 - side, "seq": core if which == 0 else other_core}
        return pltpu.make_async_remote_copy(
            src_ref=returned.at[h], dst_ref=full.at[side, h],
            send_sem=full_send.at[min(which, 1), h], recv_sem=full_recv.at[side, h],
            device_id=target, device_id_type=MESH,
        )

    def received(origin, h):
        where = full.at[origin, h]
        return pltpu.make_async_remote_copy(
            src_ref=where, dst_ref=where,
            send_sem=full_send.at[0, h], recv_sem=full_recv.at[origin, h],
            device_id={"seq": other_core}, device_id_type=MESH,
        )

    straight = side == core

    def distribute(h):
        @pl.when(straight)
        def _():
            hand_over(h, 2).start()
            full[side, h] = returned[h]

        @pl.when(jnp.logical_not(straight))
        def _():
            hand_over(h, 0).start()
            hand_over(h, 1).start()

    factor = hd ** (-0.5) * math.log2(math.e)

    def attend(rows_q, h):
        keys = held[h, :, 0].reshape(8 * rows, hd)
        values = held[h, :, 1].reshape(8 * rows, hd)
        values = jnp.concatenate([values, jnp.ones_like(values)], 1)
        half = rows // 2
        parts = []
        for start in (0, half):
            scores = lax.dot_general(
                rows_q[h, start : start + half],
                keys,
                (((1,), (1,)), ((), ())),
                preferred_element_type=jnp.float32,
            )
            weights = jnp.exp2(scores * factor).astype(jnp.bfloat16)
            total = jnp.dot(weights, values, preferred_element_type=jnp.float32)
            parts.append((total[:, :hd] / total[:, hd:]).astype(jnp.bfloat16))
        return jnp.concatenate(parts, 0)

    barrier = pltpu.get_barrier_semaphore()
    pl.semaphore_signal(barrier, inc=1, device_id={"seq": other_core}, device_id_type=MESH)
    pl.semaphore_signal(barrier, inc=1, device_id={"patch": inner}, device_id_type=MESH)

    for target in (
        {"group": 1 - group},
        {"tensor": 1 - side},
        {"tensor": 1 - side, "seq": other_core},
    ):
        pl.semaphore_signal(barrier, inc=1, device_id=target, device_id_type=MESH)

    @pl.when(is_mid)
    def _():
        pl.semaphore_signal(barrier, inc=1, device_id={"patch": outer}, device_id_type=MESH)

    row_ids = positions[:, 0:1]
    angle = row_ids * table[0:1, :] + positions[:, 1:2] * table[1:2, :]
    sine = jnp.sin(angle)
    cosine[...] = jnp.cos(angle)
    sine_low[...] = sine * table[2:3, :]
    sine_high[...] = sine * table[3:4, :]
    text = row_ids == 0
    gain_q[...] = jnp.where(text, gains[0:1, :], gains[2:3, :])
    gain_k[...] = jnp.where(text, gains[1:2, :], gains[3:4, :])
    for stream in range(2):
        gates[stream : stream + 1, :] = gate_table[stream, pl.ds(step_index[0], 1), :]

    full_mean = jnp.full((hd, hd), 1.0 / hd, jnp.float32)
    in_low = lax.broadcasted_iota(jnp.int32, (hd, hd), 0) < hd // 2
    out_low = lax.broadcasted_iota(jnp.int32, (hd, hd), 1) < hd // 2
    half_mean = jnp.where(in_low == out_low, 2.0 / hd, 0.0)
    half_len = RB // 2

    def prepare_head(h):
        place = pl.ds(pl.multiple_of(h * hd, hd), hd)
        whole = (sizes[h] == hd).astype(jnp.float32)
        grouped = (whole * full_mean + (1.0 - whole) * half_mean).astype(jnp.bfloat16)

        def embed(raw, gain):
            values = raw[:, place].astype(jnp.float32)
            mean_sq = split_dot(values * values, full_mean.astype(jnp.bfloat16))
            normed = values * lax.rsqrt(mean_sq + norm_eps) * gain[...]
            return (
                normed * cosine[...]
                + pltpu.roll(normed, hd - half_len, 1) * sine_low[...]
                + pltpu.roll(normed, half_len, 1) * sine_high[...]
            )

        def update(fresh, old):
            kept = old[:, place].astype(jnp.float32)
            residual = fresh - kept
            scale = jnp.sqrt(split_dot(residual * residual, grouped) + norm_eps)
            scale = scale.astype(jnp.bfloat16).astype(jnp.float32)
            code = jnp.tanh(residual / scale).astype(jnp.bfloat16).astype(jnp.float32)
            return (kept + scale * code).astype(jnp.bfloat16)

        key_next = update(embed(key_raw, gain_k), key_old)
        value_next = update(value_raw[:, place].astype(jnp.float32), value_old)
        held[h, slot(chip), 0] = key_next
        held[h, slot(chip), 1] = value_next
        key_out[:, place] = key_next
        value_out[:, place] = value_next
        query[h] = embed(query_raw, gain_q).astype(jnp.bfloat16)

    pl.semaphore_wait(barrier, jnp.where(is_end, 5, 6))

    def arrived(h, source):
        along(h, source, inner, in_send).wait_recv()

    def siblings(h):
        def one(source, carry):
            aside(h, source).wait_recv()
            return carry

        lax.fori_loop(0, 4, one, 0)

    def start_weights():
        @pl.when(gives_text)
        def _():
            across(0, 0).start()
            across(0, 1).start()

        @pl.when(jnp.logical_not(gives_text))
        def _():
            for c in range(CHUNKS):
                across(1, c).start()

        load(1).start()

        @pl.when(has_text)
        def _():
            load(0).start()

    @pl.when(is_end)
    def _():
        def push(h, carry):
            prepare_head(h)
            along(h, chip, inner, in_send).start()

            @pl.when(h < shared)
            def _():
                aside(h, chip).start()

            @pl.when(h >= shared)
            def _():
                lend(h).start()

            return carry

        lax.fori_loop(0, heads, push, 0)
        start_weights()

        def step(h, carry):
            for source in (my_mid, far_mid, far_end):
                arrived(h, source)
                aside(h, source).start()
            siblings(h)
            returned[h] = attend(query, h)
            distribute(h)

            @pl.when(has_text)
            def _():
                relay(0, h)

            @pl.when(jnp.logical_not(has_text))
            def _():
                relay(1, h)

            @pl.when(gives_text)
            def _():
                across(0, h).wait_send()

                @pl.when(h == 0)
                def _():
                    across(0, 2).start()

                @pl.when(h > 0)
                def _():
                    across(1, h - 1).start()

            return carry

        lax.fori_loop(0, shared, step, 0)

        def finish(h, carry):
            @pl.when(has_text)
            def _():
                relay(1, h - shared)

            @pl.when(gives_text & (h == shared))
            def _():
                across(1, 0).wait_send()
                across(1, 2).start()

            give_back(h).wait_recv()
            distribute(h)
            return carry

        lax.fori_loop(shared, heads, finish, 0)

        def drain(h, carry):
            along(h, chip, inner, in_send).wait_send()

            @pl.when(h < shared)
            def _():
                for source in (chip, my_mid, far_mid, far_end):
                    aside(h, source).wait_send()

            @pl.when(h >= shared)
            def _():
                lend(h).wait_send()

            return carry

        lax.fori_loop(0, heads, drain, 0)

    @pl.when(is_mid)
    def _():
        def push(h, carry):
            prepare_head(h)
            @pl.when(h < 2)
            def _():
                along(h, chip, inner, in_send).start()

            @pl.when(h < shared)
            def _():
                along(h, chip, outer, out_send).start()

            aside(h, chip).start()
            return carry

        lax.fori_loop(0, heads, push, 0)

        def take_end(h):
            arrived(h, my_end)
            along(h, my_end, inner, in_send).start()
            aside(h, my_end).start()

        start_weights()
        take_end(0)

        def step(h, carry):
            @pl.when(h + 2 < heads)
            def _():
                along(h + 2, chip, inner, in_send).start()

            @pl.when(h + 1 < heads)
            def _():
                take_end(h + 1)

            for source in (far_mid, far_end):
                arrived(h, source)
                aside(h, source).start()

                @pl.when(h < shared)
                def _():
                    along(h, source, outer, out_send).start()

            siblings(h)

            @pl.when(h >= shared)
            def _():
                lend(h).wait_recv()
                mixed[h] = attend(guest, h)
                give_back(h).start()

            returned[h] = attend(query, h)
            distribute(h)

            @pl.when(h < CHUNKS)
            def _():
                relay(1, h)

            return carry

        lax.fori_loop(0, heads, step, 0)

        def drain(h, carry):
            along(h, chip, inner, in_send).wait_send()
            along(h, my_end, inner, in_send).wait_send()
            for source in (chip, my_end, far_mid, far_end):
                aside(h, source).wait_send()

            @pl.when(h < shared)
            def _():
                for source in (chip, far_mid, far_end):
                    along(h, source, outer, out_send).wait_send()

            @pl.when(h >= shared)
            def _():
                give_back(h).wait_send()

            return carry

        lax.fori_loop(0, heads, drain, 0)

    load(1).wait()
    for c in range(CHUNKS):
        pass_on(1, c).wait_recv()

    @pl.when(has_text)
    def _():
        load(0).wait()
        for c in range(CHUNKS):
            pass_on(0, c).wait_recv()

    def collect(h, carry):
        received(1 - side, h).wait_recv()

        @pl.when(jnp.logical_not(straight))
        def _():
            received(side, h).wait_recv()

        return carry

    lax.fori_loop(0, heads, collect, 0)
    own_rows = jnp.concatenate([full[side, h] for h in range(heads)], 1)
    far_rows = jnp.concatenate([full[1 - side, h] for h in range(heads)], 1)
    width = 512

    def project(first, last, stream, place):
        sums = jnp.dot(
            own_rows[first:last], own_weight[stream, :, place], preferred_element_type=jnp.float32
        ) + jnp.dot(
            far_rows[first:last], far_weight[stream, :, place], preferred_element_type=jnp.float32
        )
        out[first:last, place] = (sums * gates[stream : stream + 1, place]).astype(out.dtype)

    def block(index, carry):
        place = pl.ds(pl.multiple_of(index * width, width), width)

        @pl.when(has_text)
        def _():
            project(0, text_rows, 0, place)
            project(text_rows, rows, 1, place)

        @pl.when(jnp.logical_not(has_text))
        def _():
            project(0, rows, 1, place)

        return carry

    lax.fori_loop(0, columns // width, block, 0)

    def drain_rows(h, carry):
        @pl.when(straight)
        def _():
            hand_over(h, 2).wait_send()

        @pl.when(jnp.logical_not(straight))
        def _():
            hand_over(h, 0).wait_send()
            hand_over(h, 1).wait_send()

        return carry

    lax.fori_loop(0, heads, drain_rows, 0)
    for c in range(CHUNKS):
        pass_on(1, c).wait_send()
    for c in range(1, CHUNKS):
        across(1, c).wait_send()

    @pl.when(jnp.logical_not(gives_text))
    def _():
        across(1, 0).wait_send()

    @pl.when(has_text)
    def _():
        for c in range(CHUNKS):
            pass_on(0, c).wait_send()


def on_device_line(
    query_raw,
    key_raw,
    value_raw,
    key_cache,
    value_cache,
    norm_gain,
    layout,
    group_size,
    step_index,
    gate_table,
    out_weight,
):
    rows, features = query_raw.shape
    heads = group_size.shape[0]
    hd = features // heads
    dma = pltpu.SemaphoreType.DMA
    in_vmem = pl.BlockSpec(memory_space=pltpu.VMEM)
    in_smem = pl.BlockSpec(memory_space=pltpu.SMEM)
    vmem = lambda *shape: pltpu.VMEM(shape, jnp.bfloat16)
    wide = pltpu.VMEM((rows, hd), jnp.float32)
    return pl.pallas_call(
        attend_kernel,
        out_shape=[
            jax.ShapeDtypeStruct((rows, out_weight.shape[2]), jnp.bfloat16),
            jax.ShapeDtypeStruct((rows, features), jnp.bfloat16),
            jax.ShapeDtypeStruct((rows, features), jnp.bfloat16),
        ],
        in_specs=[in_smem] * 2 + [in_vmem] * 9 + [pl.BlockSpec(memory_space=pl.ANY)],
        out_specs=[in_vmem] * 3,
        scratch_shapes=[
            vmem(heads, rows, hd),
            pltpu.VMEM((2, out_weight.shape[2]), jnp.float32),
        ]
        + [wide] * 5
        + [
            vmem(heads, 8, 2, rows, hd),
            vmem(heads, rows, hd),
            vmem(heads, rows, hd),
            vmem(heads, rows, hd),
            vmem(2, heads, rows, hd),
            vmem(*out_weight.shape),
            vmem(*out_weight.shape),
        ]
        + [dma((heads, 4))] * 5
        + [dma((heads,))] * 4
        + [dma((2, heads))] * 2
        + [dma((2, CHUNKS))] * 4
        + [dma((2,))],
        compiler_params=pltpu.CompilerParams(
            collective_id=0, has_side_effects=True, vmem_limit_bytes=60 * 2**20
        ),
    )(
        group_size,
        step_index,
        layout.astype(jnp.float32).T,
        norm_gain.reshape(4, hd),
        lane_tables(hd),
        query_raw,
        key_raw,
        value_raw,
        key_cache,
        value_cache,
        gate_table,
        out_weight,
    )


def solution(mesh):
    in_specs = (
        P(("group", "patch", "seq"), "tensor"),
        P(("group", "patch", "seq"), "tensor"),
        P(("group", "patch", "seq"), "tensor"),
        P(("group", "patch", "seq"), "tensor"),
        P(("group", "patch", "seq"), "tensor"),
        P(),
        P(None, ("group", "patch", "seq")),
        P("tensor"),
        P("group"),
        P(None, None, "seq"),
        P(None, "tensor", "seq"),
    )
    out_specs = (
        P(("group", "patch", "tensor"), "seq"),
        P(("group", "patch", "seq"), "tensor"),
        P(("group", "patch", "seq"), "tensor"),
    )
    fast = mesh.shape["patch"] == 4 and mesh.shape["tensor"] == 2 and mesh.shape["seq"] == 2
    return jax.shard_map(
        on_device_line if fast else on_device, mesh=mesh, in_specs=in_specs, out_specs=out_specs, check_vma=False
    )
```

```python
import functools
import math
import jax
import jax.numpy as jnp
import numpy as np
from jax import lax
from jax.experimental import pallas as pl
from jax.experimental.pallas import tpu as pltpu
from jax.sharding import PartitionSpec as P

RA = 16
RB = 56


rope_theta = 10000.0
norm_eps = 1e-06


def rope_tables(positions, plain_dims, rotary_dims):
    half_len = rotary_dims // 2
    exponent = jnp.arange(half_len, dtype=jnp.float32) * (2.0 / rotary_dims)
    freqs = jnp.exp(-jnp.log(rope_theta) * exponent)
    token_count = positions.shape[1]
    cosine = [jnp.ones((token_count, plain_dims), jnp.float32)]
    sine_part = [jnp.zeros((token_count, plain_dims), jnp.float32)]
    for which in range(2):
        angle = positions[which].astype(jnp.float32)[:, None] * freqs[None, :]
        cosine += [jnp.cos(angle), jnp.cos(angle)]
        sine_part += [jnp.sin(angle), jnp.sin(angle)]
    return (jnp.concatenate(cosine, 1), jnp.concatenate(sine_part, 1))


def partner(values, plain_dims, rotary_dims):
    half_len = rotary_dims // 2
    second = plain_dims + rotary_dims
    return jnp.concatenate(
        [
            values[..., :plain_dims],
            -values[..., plain_dims + half_len : second],
            values[..., plain_dims : plain_dims + half_len],
            -values[..., second + half_len :],
            values[..., second : second + half_len],
        ],
        -1,
    )


def compress(residual, group_size, heads, head_dim):
    row_count = residual.shape[0]
    halves = residual.reshape(row_count, heads, 2, head_dim // 2)
    half_ms = jnp.mean(halves * halves, -1)
    whole_ms = jnp.mean(half_ms, -1, keepdims=True)
    whole = (group_size == head_dim)[None, :, None]
    mean_sq = jnp.where(whole, whole_ms, half_ms)
    scales = jnp.sqrt(mean_sq + norm_eps).astype(jnp.bfloat16)
    codes = jnp.tanh(halves / scales.astype(jnp.float32)[..., None]).astype(jnp.bfloat16)
    return (codes.reshape(row_count, heads * head_dim), scales.reshape(row_count, heads * 2))


def decode(codes, scales, heads, head_dim):
    row_count = codes.shape[0]
    parts = codes.astype(jnp.float32).reshape(row_count, heads, 2, head_dim // 2) * scales.astype(
        jnp.float32
    ).reshape(row_count, heads, 2, 1)
    return parts.reshape(row_count, heads * head_dim)


def prepare(query_raw, key_raw, value_raw, positions, norm_gain, key_rows, value_rows, group_size):
    row_count = query_raw.shape[0]
    heads = group_size.shape[0]
    head_dim = norm_gain.shape[-1]
    text_rows = (positions[0] == 0)[:, None, None]
    cosine, sine_part = rope_tables(positions, RA, RB)
    cosine = cosine[:, None, :]
    sine_part = sine_part[:, None, :]

    def embed(raw, which):
        gain = jnp.where(
            text_rows, norm_gain[0, which][None, None, :], norm_gain[1, which][None, None, :]
        )
        values = raw.astype(jnp.float32).reshape(row_count, heads, head_dim)
        normed = values * lax.rsqrt(jnp.mean(values * values, -1, keepdims=True) + norm_eps) * gain
        return (normed * cosine + partner(normed, RA, RB) * sine_part).reshape(
            row_count, heads * head_dim
        )

    query_rot = embed(query_raw, 0).astype(jnp.bfloat16)
    key_rot = embed(key_raw, 1)
    key_codes, key_scales = compress(
        key_rot - key_rows.astype(jnp.float32), group_size, heads, head_dim
    )
    value_codes, value_scales = compress(
        value_raw.astype(jnp.float32) - value_rows.astype(jnp.float32), group_size, heads, head_dim
    )
    return (query_rot, key_codes, value_codes, key_scales, value_scales)


def block_length(piece_rows):
    for candidate in range(min(piece_rows, 2048), 0, -1):
        if piece_rows % candidate == 0:
            return candidate
    return piece_rows


def on_device(
    query_raw,
    key_raw,
    value_raw,
    key_cache,
    value_cache,
    norm_gain,
    layout,
    group_size,
    step_index,
    gate_table,
    out_weight,
):
    row_count = query_raw.shape[0]
    heads = group_size.shape[0]
    head_dim = norm_gain.shape[-1]
    query_rot, key_codes, value_codes, key_scales, value_scales = prepare(
        query_raw, key_raw, value_raw, layout, norm_gain, key_cache, value_cache, group_size
    )
    key_mine = (
        key_cache.astype(jnp.float32) + decode(key_codes, key_scales, heads, head_dim)
    ).astype(jnp.bfloat16)
    value_mine = (
        value_cache.astype(jnp.float32) + decode(value_codes, value_scales, heads, head_dim)
    ).astype(jnp.bfloat16)
    query_heads = query_rot.reshape(row_count, heads, head_dim)
    inverse_root = head_dim ** (-0.5)
    start_state = (
        jnp.zeros((heads, row_count, head_dim), jnp.float32),
        jnp.zeros((heads, row_count), jnp.float32),
    )
    keys_all = lax.all_gather(key_mine, ("patch", "seq"), axis=0, tiled=True)
    values_all = lax.all_gather(value_mine, ("patch", "seq"), axis=0, tiled=True)
    piece_rows = keys_all.shape[0]
    length = block_length(piece_rows)

    def one_block(index, carry):
        numer, totals = carry
        keys = lax.dynamic_slice_in_dim(keys_all, index * length, length, 0).reshape(
            length, heads, head_dim
        )
        values = lax.dynamic_slice_in_dim(values_all, index * length, length, 0).reshape(
            length, heads, head_dim
        )
        scores = (
            jnp.einsum("qhd,khd->hqk", query_heads, keys, preferred_element_type=jnp.float32)
            * inverse_root
        )
        weights = jnp.exp(scores)
        totals = totals + jnp.sum(weights, -1)
        numer = numer + jnp.einsum(
            "hqk,khd->hqd", weights.astype(jnp.bfloat16), values, preferred_element_type=jnp.float32
        )
        return (numer, totals)

    numer, totals = lax.fori_loop(0, piece_rows // length, one_block, start_state)
    attn_rows = (
        (numer / totals[..., None])
        .transpose(1, 0, 2)
        .reshape(row_count, heads * head_dim)
        .astype(jnp.bfloat16)
    )
    text_flag = (layout[0] == 0).astype(jnp.bfloat16)
    pair_attn, pair_text = (
        lax.all_gather(attn_rows, "seq", axis=0, tiled=True),
        lax.all_gather(text_flag, "seq", axis=0, tiled=True),
    )
    share = pair_attn.shape[0] // lax.axis_size("tensor")

    def both_streams(block, block_text):
        text_part = jnp.dot(block, out_weight[0], preferred_element_type=jnp.float32)
        image_part = jnp.dot(block, out_weight[1], preferred_element_type=jnp.float32)
        return jnp.where(block_text[:, None] > 0, text_part, image_part)

    def image_only(block, block_text):
        return jnp.dot(block, out_weight[1], preferred_element_type=jnp.float32)

    block = pair_attn
    block_text = pair_text
    projected = lax.psum_scatter(
        lax.cond(jnp.any(block_text > 0), both_streams, image_only, block, block_text),
        "tensor",
        scatter_dimension=0,
        tiled=True,
    )
    mine_text = lax.dynamic_slice_in_dim(pair_text, lax.axis_index("tensor") * share, share, 0)
    chosen = (jnp.arange(gate_table.shape[1]) == step_index[0]).astype(jnp.float32)
    gates = jnp.sum(gate_table * chosen[None, :, None], 1)
    gate_rows = jnp.where(mine_text[:, None] > 0, gates[0][None, :], gates[1][None, :])
    return ((gate_rows * projected).astype(jnp.bfloat16), key_mine, value_mine)


MESH = pl.DeviceIdType.MESH
GATHER_SHARE = 2
CHUNKS = 3
TEXT_PART = 12


def lane_tables(head_dim):
    half_len = RB // 2
    freqs = np.exp(-math.log(rope_theta) * np.arange(half_len) * (2.0 / RB)).astype(np.float32)
    table = np.zeros((8, head_dim), np.float32)
    for which in range(2):
        start = RA + which * RB
        table[which, start : start + half_len] = freqs
        table[which, start + half_len : start + RB] = freqs
        table[2, start : start + half_len] = -1.0
        table[3, start + half_len : start + RB] = 1.0
    return jnp.asarray(table)


def split_dot(values, matrix):
    high = values.astype(jnp.bfloat16)
    low = (values - high.astype(jnp.float32)).astype(jnp.bfloat16)
    return jnp.dot(
        jnp.concatenate([high, low], 1),
        jnp.concatenate([matrix, matrix], 0),
        preferred_element_type=jnp.float32,
    )


def attend_kernel(
    sizes, step_index, positions, gains, table, query_raw, key_raw, value_raw, key_old, value_old,
    gate_table, weight, out, key_out, value_out, query, gates, cosine, sine_low, sine_high,
    gain_q, gain_k, held, guest, mixed, returned, full, own_weight, far_weight,
    in_send, out_send, side_send, line_recv, side_recv, guest_send, guest_recv, back_send,
    back_recv, full_send, full_recv, across_send, across_recv, group_send, group_recv, load_sem,
    lent_rows, part_out, part_in, lent_send, lent_recv, part_sem,
):
    heads, rows, hd = query.shape
    features, columns = weight.shape[1:]
    group = lax.axis_index("group")
    side = lax.axis_index("tensor")
    shared = heads // GATHER_SHARE
    chip = lax.axis_index("patch")
    core = lax.axis_index("seq")
    other_core = 1 - core
    upper = chip // 2
    is_end = (chip == 0) | (chip == 3)
    is_mid = jnp.logical_not(is_end)
    my_end = upper * 3
    my_mid = 1 + upper
    far_mid = 2 - upper
    far_end = 3 - my_end
    inner = jnp.where(is_end, my_mid, far_mid)
    outer = my_end

    def slot(source):
        return source * 2 + core

    def to_chip(src, dst, send, recv, target):
        return pltpu.make_async_remote_copy(
            src_ref=src, dst_ref=dst, send_sem=send, recv_sem=recv,
            device_id={"patch": target}, device_id_type=MESH,
        )

    def along(h, source, target, send):
        where = held.at[h, slot(source)]
        return to_chip(where, where, send.at[h, source], line_recv.at[h, source], target)

    def aside(h, source):
        where = held.at[h, slot(source)]
        return pltpu.make_async_remote_copy(
            src_ref=where, dst_ref=where, send_sem=side_send.at[h, source],
            recv_sem=side_recv.at[h, source],
            device_id={"seq": other_core}, device_id_type=MESH,
        )

    def lend(h):
        return to_chip(
            query.at[h], guest.at[h], guest_send.at[h], guest_recv.at[h], inner
        )

    def give_back(h):
        return to_chip(
            mixed.at[h], returned.at[h], back_send.at[h], back_recv.at[h], outer
        )

    has_text = (chip == 0) & (side == 0)
    gives_text = (chip == 0) & (side == 1)
    text_rows = rows * 8 // TEXT_PART
    chunk = features // 2 // CHUNKS

    def weight_rows(owner, c):
        return pl.ds(pl.multiple_of(owner * (features // 2) + c * chunk, chunk), chunk)

    def across(stream, c):
        where = weight_rows(group, c)
        return pltpu.make_async_remote_copy(
            src_ref=weight.at[stream, where], dst_ref=far_weight.at[stream, where],
            send_sem=across_send.at[stream, c], recv_sem=across_recv.at[stream, c],
            device_id={"tensor": 1 - side}, device_id_type=MESH,
        )

    def pass_on(stream, c):
        where = far_weight.at[stream, weight_rows(group, c)]
        return pltpu.make_async_remote_copy(
            src_ref=where, dst_ref=where,
            send_sem=group_send.at[stream, c], recv_sem=group_recv.at[stream, c],
            device_id={"group": 1 - group}, device_id_type=MESH,
        )

    def relay(stream, c):
        across(stream, c).wait_recv()
        pass_on(stream, c).start()

    def load(stream):
        return pltpu.make_async_copy(
            weight.at[stream], own_weight.at[stream], load_sem.at[stream]
        )

    def hand_over(h, which):
        if which == 2:
            target = {"seq": other_core}
        else:
            target = {"tensor": 1 - side, "seq": core if which == 0 else other_core}
        return pltpu.make_async_remote_copy(
            src_ref=returned.at[h], dst_ref=full.at[side, h],
            send_sem=full_send.at[min(which, 1), h], recv_sem=full_recv.at[side, h],
            device_id=target, device_id_type=MESH,
        )

    def received(origin, h):
        where = full.at[origin, h]
        return pltpu.make_async_remote_copy(
            src_ref=where, dst_ref=where,
            send_sem=full_send.at[0, h], recv_sem=full_recv.at[origin, h],
            device_id={"seq": other_core}, device_id_type=MESH,
        )

    straight = side == core
    image_rows = pl.ds(text_rows, rows - text_rows)

    def lend_rows(h):
        return pltpu.make_async_remote_copy(
            src_ref=returned.at[h, image_rows], dst_ref=lent_rows.at[h],
            send_sem=lent_send.at[h], recv_sem=lent_recv.at[h],
            device_id={"seq": other_core}, device_id_type=MESH,
        )

    def send_part():
        return pltpu.make_async_remote_copy(
            src_ref=part_out, dst_ref=part_in,
            send_sem=part_sem.at[0], recv_sem=part_sem.at[1],
            device_id={"tensor": 1 - side}, device_id_type=MESH,
        )

    def distribute(h):
        @pl.when(straight)
        def _():
            hand_over(h, 2).start()
            full[side, h] = returned[h]

        @pl.when(jnp.logical_not(straight))
        def _():
            hand_over(h, 0).start()
            hand_over(h, 1).start()

        @pl.when(gives_text & (core == 0))
        def _():
            lend_rows(h).start()

    factor = hd ** (-0.5) * math.log2(math.e)

    def attend(rows_q, h):
        keys = held[h, :, 0].reshape(8 * rows, hd)
        values = held[h, :, 1].reshape(8 * rows, hd)
        values = jnp.concatenate([values, jnp.ones_like(values)], 1)
        half = rows // 2
        parts = []
        for start in (0, half):
            scores = lax.dot_general(
                rows_q[h, start : start + half],
                keys,
                (((1,), (1,)), ((), ())),
                preferred_element_type=jnp.float32,
            )
            weights = jnp.exp2(scores * factor).astype(jnp.bfloat16)
            total = jnp.dot(weights, values, preferred_element_type=jnp.float32)
            parts.append((total[:, :hd] / total[:, hd:]).astype(jnp.bfloat16))
        return jnp.concatenate(parts, 0)

    barrier = pltpu.get_barrier_semaphore()
    pl.semaphore_signal(barrier, inc=1, device_id={"seq": other_core}, device_id_type=MESH)
    pl.semaphore_signal(barrier, inc=1, device_id={"patch": inner}, device_id_type=MESH)

    for target in (
        {"group": 1 - group},
        {"tensor": 1 - side},
        {"tensor": 1 - side, "seq": other_core},
    ):
        pl.semaphore_signal(barrier, inc=1, device_id=target, device_id_type=MESH)

    @pl.when(is_mid)
    def _():
        pl.semaphore_signal(barrier, inc=1, device_id={"patch": outer}, device_id_type=MESH)

    row_ids = positions[:, 0:1]
    angle = row_ids * table[0:1, :] + positions[:, 1:2] * table[1:2, :]
    sine = jnp.sin(angle)
    cosine[...] = jnp.cos(angle)
    sine_low[...] = sine * table[2:3, :]
    sine_high[...] = sine * table[3:4, :]
    text = row_ids == 0
    gain_q[...] = jnp.where(text, gains[0:1, :], gains[2:3, :])
    gain_k[...] = jnp.where(text, gains[1:2, :], gains[3:4, :])
    for stream in range(2):
        gates[stream : stream + 1, :] = gate_table[stream, pl.ds(step_index[0], 1), :]

    full_mean = jnp.full((hd, hd), 1.0 / hd, jnp.float32)
    in_low = lax.broadcasted_iota(jnp.int32, (hd, hd), 0) < hd // 2
    out_low = lax.broadcasted_iota(jnp.int32, (hd, hd), 1) < hd // 2
    half_mean = jnp.where(in_low == out_low, 2.0 / hd, 0.0)
    half_len = RB // 2

    def prepare_head(h):
        place = pl.ds(pl.multiple_of(h * hd, hd), hd)
        whole = (sizes[h] == hd).astype(jnp.float32)
        grouped = (whole * full_mean + (1.0 - whole) * half_mean).astype(jnp.bfloat16)

        def embed(raw, gain):
            values = raw[:, place].astype(jnp.float32)
            mean_sq = split_dot(values * values, full_mean.astype(jnp.bfloat16))
            normed = values * lax.rsqrt(mean_sq + norm_eps) * gain[...]
            return (
                normed * cosine[...]
                + pltpu.roll(normed, hd - half_len, 1) * sine_low[...]
                + pltpu.roll(normed, half_len, 1) * sine_high[...]
            )

        def update(fresh, old):
            kept = old[:, place].astype(jnp.float32)
            residual = fresh - kept
            scale = jnp.sqrt(split_dot(residual * residual, grouped) + norm_eps)
            scale = scale.astype(jnp.bfloat16).astype(jnp.float32)
            code = jnp.tanh(residual / scale).astype(jnp.bfloat16).astype(jnp.float32)
            return (kept + scale * code).astype(jnp.bfloat16)

        key_next = update(embed(key_raw, gain_k), key_old)
        value_next = update(value_raw[:, place].astype(jnp.float32), value_old)
        held[h, slot(chip), 0] = key_next
        held[h, slot(chip), 1] = value_next
        key_out[:, place] = key_next
        value_out[:, place] = value_next
        query[h] = embed(query_raw, gain_q).astype(jnp.bfloat16)

    pl.semaphore_wait(barrier, jnp.where(is_end, 5, 6))

    def arrived(h, source):
        along(h, source, inner, in_send).wait_recv()

    def siblings(h):
        def one(source, carry):
            aside(h, source).wait_recv()
            return carry

        lax.fori_loop(0, 4, one, 0)

    def start_weights():
        for c in range(CHUNKS):
            @pl.when(gives_text)
            def _():
                across(0, c).start()

            @pl.when(jnp.logical_not(gives_text))
            def _():
                across(1, c).start()

        load(1).start()

        @pl.when(has_text)
        def _():
            load(0).start()

    start_weights()

    @pl.when(is_end)
    def _():
        def push(h, carry):
            prepare_head(h)
            along(h, chip, inner, in_send).start()

            @pl.when(h < shared)
            def _():
                aside(h, chip).start()

            @pl.when(h >= shared)
            def _():
                lend(h).start()

            return carry

        lax.fori_loop(0, heads, push, 0)

        def step(h, carry):
            for source in (my_mid, far_mid, far_end):
                arrived(h, source)
                aside(h, source).start()
            siblings(h)
            returned[h] = attend(query, h)
            distribute(h)

            @pl.when(has_text)
            def _():
                relay(0, h)

            @pl.when(jnp.logical_not(has_text))
            def _():
                relay(1, h)

            return carry

        lax.fori_loop(0, shared, step, 0)

        def finish(h, carry):
            give_back(h).wait_recv()
            distribute(h)
            return carry

        lax.fori_loop(shared, heads, finish, 0)

        def drain(h, carry):
            along(h, chip, inner, in_send).wait_send()

            @pl.when(h < shared)
            def _():
                for source in (chip, my_mid, far_mid, far_end):
                    aside(h, source).wait_send()

            @pl.when(h >= shared)
            def _():
                lend(h).wait_send()

            return carry

        lax.fori_loop(0, heads, drain, 0)

    @pl.when(is_mid)
    def _():
        def push(h, carry):
            prepare_head(h)
            @pl.when(h < 2)
            def _():
                along(h, chip, inner, in_send).start()

            @pl.when(h < shared)
            def _():
                along(h, chip, outer, out_send).start()

            aside(h, chip).start()
            return carry

        lax.fori_loop(0, heads, push, 0)

        def take_end(h):
            arrived(h, my_end)
            along(h, my_end, inner, in_send).start()
            aside(h, my_end).start()

        take_end(0)

        def step(h, carry):
            @pl.when(h + 2 < heads)
            def _():
                along(h + 2, chip, inner, in_send).start()

            @pl.when(h + 1 < heads)
            def _():
                take_end(h + 1)

            for source in (far_mid, far_end):
                arrived(h, source)
                aside(h, source).start()

                @pl.when(h < shared)
                def _():
                    along(h, source, outer, out_send).start()

            siblings(h)

            @pl.when(h >= shared)
            def _():
                lend(h).wait_recv()
                mixed[h] = attend(guest, h)
                give_back(h).start()

            returned[h] = attend(query, h)
            distribute(h)

            @pl.when(h < CHUNKS)
            def _():
                relay(1, h)

            return carry

        lax.fori_loop(0, heads, step, 0)

        def drain(h, carry):
            along(h, chip, inner, in_send).wait_send()
            along(h, my_end, inner, in_send).wait_send()
            for source in (chip, my_end, far_mid, far_end):
                aside(h, source).wait_send()

            @pl.when(h < shared)
            def _():
                for source in (chip, far_mid, far_end):
                    along(h, source, outer, out_send).wait_send()

            @pl.when(h >= shared)
            def _():
                give_back(h).wait_send()

            return carry

        lax.fori_loop(0, heads, drain, 0)

    width = 512
    load(1).wait()

    @pl.when(gives_text)
    def _():
        @pl.when(core == 0)
        def _():
            for h in range(heads):
                lent_rows[h] = returned[h, text_rows:]

        @pl.when(core == 1)
        def _():
            for h in range(heads):
                lend_rows(h).wait_recv()

        partial_rows = jnp.concatenate([lent_rows[h] for h in range(heads)], 1)
        for first in range(0, columns, width):
            part_out[:, first : first + width] = jnp.dot(
                partial_rows,
                own_weight[1, :, first : first + width],
                preferred_element_type=jnp.float32,
            ).astype(part_out.dtype)
        send_part().start()

    @pl.when(jnp.logical_not(has_text))
    def _():
        for c in range(CHUNKS):
            pass_on(1, c).wait_recv()

    @pl.when(has_text)
    def _():
        load(0).wait()
        for c in range(CHUNKS):
            pass_on(0, c).wait_recv()

    def collect(h, carry):
        received(1 - side, h).wait_recv()

        @pl.when(jnp.logical_not(straight))
        def _():
            received(side, h).wait_recv()

        return carry

    lax.fori_loop(0, heads, collect, 0)
    own_rows = jnp.concatenate([full[side, h] for h in range(heads)], 1)
    far_rows = jnp.concatenate([full[1 - side, h] for h in range(heads)], 1)
    @pl.when(has_text)
    def _():
        send_part().wait_recv()

    def project(first, last, stream, place):
        sums = jnp.dot(
            own_rows[first:last], own_weight[stream, :, place], preferred_element_type=jnp.float32
        ) + jnp.dot(
            far_rows[first:last], far_weight[stream, :, place], preferred_element_type=jnp.float32
        )
        out[first:last, place] = (sums * gates[stream : stream + 1, place]).astype(out.dtype)

    def block(index, carry):
        place = pl.ds(pl.multiple_of(index * width, width), width)

        @pl.when(has_text)
        def _():
            project(0, text_rows, 0, place)
            sums = jnp.dot(
                own_rows[text_rows:], own_weight[1, :, place], preferred_element_type=jnp.float32
            ) + part_in[:, place].astype(jnp.float32)
            out[text_rows:, place] = (sums * gates[1:2, place]).astype(out.dtype)

        @pl.when(jnp.logical_not(has_text))
        def _():
            project(0, rows, 1, place)

        return carry

    lax.fori_loop(0, columns // width, block, 0)

    def drain_rows(h, carry):
        @pl.when(straight)
        def _():
            hand_over(h, 2).wait_send()

        @pl.when(jnp.logical_not(straight))
        def _():
            hand_over(h, 0).wait_send()
            hand_over(h, 1).wait_send()

        return carry

    lax.fori_loop(0, heads, drain_rows, 0)
    for c in range(CHUNKS):
        @pl.when(gives_text)
        def _():
            across(0, c).wait_send()

        @pl.when(jnp.logical_not(gives_text))
        def _():
            across(1, c).wait_send()

        @pl.when(has_text)
        def _():
            pass_on(0, c).wait_send()

        @pl.when(jnp.logical_not(has_text))
        def _():
            pass_on(1, c).wait_send()

    @pl.when(gives_text)
    def _():
        send_part().wait_send()

        @pl.when(core == 0)
        def _():
            for h in range(heads):
                lend_rows(h).wait_send()


def on_device_line(
    query_raw,
    key_raw,
    value_raw,
    key_cache,
    value_cache,
    norm_gain,
    layout,
    group_size,
    step_index,
    gate_table,
    out_weight,
):
    rows, features = query_raw.shape
    heads = group_size.shape[0]
    hd = features // heads
    text_rows = rows * 8 // TEXT_PART
    dma = pltpu.SemaphoreType.DMA
    in_vmem = pl.BlockSpec(memory_space=pltpu.VMEM)
    in_smem = pl.BlockSpec(memory_space=pltpu.SMEM)
    vmem = lambda *shape: pltpu.VMEM(shape, jnp.bfloat16)
    wide = pltpu.VMEM((rows, hd), jnp.float32)
    return pl.pallas_call(
        attend_kernel,
        out_shape=[
            jax.ShapeDtypeStruct((rows, out_weight.shape[2]), jnp.bfloat16),
            jax.ShapeDtypeStruct((rows, features), jnp.bfloat16),
            jax.ShapeDtypeStruct((rows, features), jnp.bfloat16),
        ],
        in_specs=[in_smem] * 2 + [in_vmem] * 9 + [pl.BlockSpec(memory_space=pl.ANY)],
        out_specs=[in_vmem] * 3,
        scratch_shapes=[
            vmem(heads, rows, hd),
            pltpu.VMEM((2, out_weight.shape[2]), jnp.float32),
        ]
        + [wide] * 5
        + [
            vmem(heads, 8, 2, rows, hd),
            vmem(heads, rows, hd),
            vmem(heads, rows, hd),
            vmem(heads, rows, hd),
            vmem(2, heads, rows, hd),
            vmem(*out_weight.shape),
            vmem(*out_weight.shape),
        ]
        + [dma((heads, 4))] * 5
        + [dma((heads,))] * 4
        + [dma((2, heads))] * 2
        + [dma((2, CHUNKS))] * 4
        + [dma((2,))]
        + [
            vmem(heads, rows - text_rows, hd),
            vmem(rows - text_rows, out_weight.shape[2]),
            vmem(rows - text_rows, out_weight.shape[2]),
        ]
        + [dma((heads,))] * 2
        + [dma((2,))],
        compiler_params=pltpu.CompilerParams(
            collective_id=0, has_side_effects=True, vmem_limit_bytes=60 * 2**20
        ),
    )(
        group_size,
        step_index,
        layout.astype(jnp.float32).T,
        norm_gain.reshape(4, hd),
        lane_tables(hd),
        query_raw,
        key_raw,
        value_raw,
        key_cache,
        value_cache,
        gate_table,
        out_weight,
    )


def solution(mesh):
    in_specs = (
        P(("group", "patch", "seq"), "tensor"),
        P(("group", "patch", "seq"), "tensor"),
        P(("group", "patch", "seq"), "tensor"),
        P(("group", "patch", "seq"), "tensor"),
        P(("group", "patch", "seq"), "tensor"),
        P(),
        P(None, ("group", "patch", "seq")),
        P("tensor"),
        P("group"),
        P(None, None, "seq"),
        P(None, "tensor", "seq"),
    )
    out_specs = (
        P(("group", "patch", "tensor"), "seq"),
        P(("group", "patch", "seq"), "tensor"),
        P(("group", "patch", "seq"), "tensor"),
    )
    fast = mesh.shape["patch"] == 4 and mesh.shape["tensor"] == 2 and mesh.shape["seq"] == 2
    return jax.shard_map(
        on_device_line if fast else on_device, mesh=mesh, in_specs=in_specs, out_specs=out_specs, check_vma=False
    )
```

```python
import functools
import math
import jax
import jax.numpy as jnp
import numpy as np
from jax import lax
from jax.experimental import pallas as pl
from jax.experimental.pallas import tpu as pltpu
from jax.sharding import PartitionSpec as P

RA = 16
RB = 56


rope_theta = 10000.0
norm_eps = 1e-06


def rope_tables(positions, plain_dims, rotary_dims):
    half_len = rotary_dims // 2
    exponent = jnp.arange(half_len, dtype=jnp.float32) * (2.0 / rotary_dims)
    freqs = jnp.exp(-jnp.log(rope_theta) * exponent)
    token_count = positions.shape[1]
    cosine = [jnp.ones((token_count, plain_dims), jnp.float32)]
    sine_part = [jnp.zeros((token_count, plain_dims), jnp.float32)]
    for which in range(2):
        angle = positions[which].astype(jnp.float32)[:, None] * freqs[None, :]
        cosine += [jnp.cos(angle), jnp.cos(angle)]
        sine_part += [jnp.sin(angle), jnp.sin(angle)]
    return (jnp.concatenate(cosine, 1), jnp.concatenate(sine_part, 1))


def partner(values, plain_dims, rotary_dims):
    half_len = rotary_dims // 2
    second = plain_dims + rotary_dims
    return jnp.concatenate(
        [
            values[..., :plain_dims],
            -values[..., plain_dims + half_len : second],
            values[..., plain_dims : plain_dims + half_len],
            -values[..., second + half_len :],
            values[..., second : second + half_len],
        ],
        -1,
    )


def compress(residual, group_size, heads, head_dim):
    row_count = residual.shape[0]
    halves = residual.reshape(row_count, heads, 2, head_dim // 2)
    half_ms = jnp.mean(halves * halves, -1)
    whole_ms = jnp.mean(half_ms, -1, keepdims=True)
    whole = (group_size == head_dim)[None, :, None]
    mean_sq = jnp.where(whole, whole_ms, half_ms)
    scales = jnp.sqrt(mean_sq + norm_eps).astype(jnp.bfloat16)
    codes = jnp.tanh(halves / scales.astype(jnp.float32)[..., None]).astype(jnp.bfloat16)
    return (codes.reshape(row_count, heads * head_dim), scales.reshape(row_count, heads * 2))


def decode(codes, scales, heads, head_dim):
    row_count = codes.shape[0]
    parts = codes.astype(jnp.float32).reshape(row_count, heads, 2, head_dim // 2) * scales.astype(
        jnp.float32
    ).reshape(row_count, heads, 2, 1)
    return parts.reshape(row_count, heads * head_dim)


def prepare(query_raw, key_raw, value_raw, positions, norm_gain, key_rows, value_rows, group_size):
    row_count = query_raw.shape[0]
    heads = group_size.shape[0]
    head_dim = norm_gain.shape[-1]
    text_rows = (positions[0] == 0)[:, None, None]
    cosine, sine_part = rope_tables(positions, RA, RB)
    cosine = cosine[:, None, :]
    sine_part = sine_part[:, None, :]

    def embed(raw, which):
        gain = jnp.where(
            text_rows, norm_gain[0, which][None, None, :], norm_gain[1, which][None, None, :]
        )
        values = raw.astype(jnp.float32).reshape(row_count, heads, head_dim)
        normed = values * lax.rsqrt(jnp.mean(values * values, -1, keepdims=True) + norm_eps) * gain
        return (normed * cosine + partner(normed, RA, RB) * sine_part).reshape(
            row_count, heads * head_dim
        )

    query_rot = embed(query_raw, 0).astype(jnp.bfloat16)
    key_rot = embed(key_raw, 1)
    key_codes, key_scales = compress(
        key_rot - key_rows.astype(jnp.float32), group_size, heads, head_dim
    )
    value_codes, value_scales = compress(
        value_raw.astype(jnp.float32) - value_rows.astype(jnp.float32), group_size, heads, head_dim
    )
    return (query_rot, key_codes, value_codes, key_scales, value_scales)


def block_length(piece_rows):
    for candidate in range(min(piece_rows, 2048), 0, -1):
        if piece_rows % candidate == 0:
            return candidate
    return piece_rows


def on_device(
    query_raw,
    key_raw,
    value_raw,
    key_cache,
    value_cache,
    norm_gain,
    layout,
    group_size,
    step_index,
    gate_table,
    out_weight,
):
    row_count = query_raw.shape[0]
    heads = group_size.shape[0]
    head_dim = norm_gain.shape[-1]
    query_rot, key_codes, value_codes, key_scales, value_scales = prepare(
        query_raw, key_raw, value_raw, layout, norm_gain, key_cache, value_cache, group_size
    )
    key_mine = (
        key_cache.astype(jnp.float32) + decode(key_codes, key_scales, heads, head_dim)
    ).astype(jnp.bfloat16)
    value_mine = (
        value_cache.astype(jnp.float32) + decode(value_codes, value_scales, heads, head_dim)
    ).astype(jnp.bfloat16)
    query_heads = query_rot.reshape(row_count, heads, head_dim)
    inverse_root = head_dim ** (-0.5)
    start_state = (
        jnp.zeros((heads, row_count, head_dim), jnp.float32),
        jnp.zeros((heads, row_count), jnp.float32),
    )
    keys_all = lax.all_gather(key_mine, ("patch", "seq"), axis=0, tiled=True)
    values_all = lax.all_gather(value_mine, ("patch", "seq"), axis=0, tiled=True)
    piece_rows = keys_all.shape[0]
    length = block_length(piece_rows)

    def one_block(index, carry):
        numer, totals = carry
        keys = lax.dynamic_slice_in_dim(keys_all, index * length, length, 0).reshape(
            length, heads, head_dim
        )
        values = lax.dynamic_slice_in_dim(values_all, index * length, length, 0).reshape(
            length, heads, head_dim
        )
        scores = (
            jnp.einsum("qhd,khd->hqk", query_heads, keys, preferred_element_type=jnp.float32)
            * inverse_root
        )
        weights = jnp.exp(scores)
        totals = totals + jnp.sum(weights, -1)
        numer = numer + jnp.einsum(
            "hqk,khd->hqd", weights.astype(jnp.bfloat16), values, preferred_element_type=jnp.float32
        )
        return (numer, totals)

    numer, totals = lax.fori_loop(0, piece_rows // length, one_block, start_state)
    attn_rows = (
        (numer / totals[..., None])
        .transpose(1, 0, 2)
        .reshape(row_count, heads * head_dim)
        .astype(jnp.bfloat16)
    )
    text_flag = (layout[0] == 0).astype(jnp.bfloat16)
    pair_attn, pair_text = (
        lax.all_gather(attn_rows, "seq", axis=0, tiled=True),
        lax.all_gather(text_flag, "seq", axis=0, tiled=True),
    )
    share = pair_attn.shape[0] // lax.axis_size("tensor")

    def both_streams(block, block_text):
        text_part = jnp.dot(block, out_weight[0], preferred_element_type=jnp.float32)
        image_part = jnp.dot(block, out_weight[1], preferred_element_type=jnp.float32)
        return jnp.where(block_text[:, None] > 0, text_part, image_part)

    def image_only(block, block_text):
        return jnp.dot(block, out_weight[1], preferred_element_type=jnp.float32)

    block = pair_attn
    block_text = pair_text
    projected = lax.psum_scatter(
        lax.cond(jnp.any(block_text > 0), both_streams, image_only, block, block_text),
        "tensor",
        scatter_dimension=0,
        tiled=True,
    )
    mine_text = lax.dynamic_slice_in_dim(pair_text, lax.axis_index("tensor") * share, share, 0)
    chosen = (jnp.arange(gate_table.shape[1]) == step_index[0]).astype(jnp.float32)
    gates = jnp.sum(gate_table * chosen[None, :, None], 1)
    gate_rows = jnp.where(mine_text[:, None] > 0, gates[0][None, :], gates[1][None, :])
    return ((gate_rows * projected).astype(jnp.bfloat16), key_mine, value_mine)


MESH = pl.DeviceIdType.MESH
GATHER_SHARE = 2
CHUNKS = 3
TEXT_PART = 12


def lane_tables(head_dim):
    half_len = RB // 2
    freqs = np.exp(-math.log(rope_theta) * np.arange(half_len) * (2.0 / RB)).astype(np.float32)
    table = np.zeros((8, head_dim), np.float32)
    for which in range(2):
        start = RA + which * RB
        table[which, start : start + half_len] = freqs
        table[which, start + half_len : start + RB] = freqs
        table[2, start : start + half_len] = -1.0
        table[3, start + half_len : start + RB] = 1.0
    return jnp.asarray(table)


def split_dot(values, matrix):
    high = values.astype(jnp.bfloat16)
    low = (values - high.astype(jnp.float32)).astype(jnp.bfloat16)
    return jnp.dot(
        jnp.concatenate([high, low], 1),
        jnp.concatenate([matrix, matrix], 0),
        preferred_element_type=jnp.float32,
    )


def attend_kernel(
    sizes, positions, gains, table, query_raw, key_raw, value_raw, key_old, value_old,
    gates, weight, out, key_out, value_out, query, cosine, sine_low, sine_high,
    gain_q, gain_k, held, guest, mixed, returned, full, own_weight, far_weight,
    in_send, out_send, side_send, line_recv, side_recv, guest_send, guest_recv, back_send,
    back_recv, full_send, full_recv, across_send, across_recv, group_send, group_recv, load_sem,
    lent_rows, part_out, part_in, lent_send, lent_recv, part_sem,
):
    heads, rows, hd = query.shape
    features, columns = weight.shape[1:]
    group = lax.axis_index("group")
    side = lax.axis_index("tensor")
    shared = heads // GATHER_SHARE
    chip = lax.axis_index("patch")
    core = lax.axis_index("seq")
    other_core = 1 - core
    upper = chip // 2
    is_end = (chip == 0) | (chip == 3)
    is_mid = jnp.logical_not(is_end)
    my_end = upper * 3
    my_mid = 1 + upper
    far_mid = 2 - upper
    far_end = 3 - my_end
    inner = jnp.where(is_end, my_mid, far_mid)
    outer = my_end

    def slot(source):
        return source * 2 + core

    def to_chip(src, dst, send, recv, target):
        return pltpu.make_async_remote_copy(
            src_ref=src, dst_ref=dst, send_sem=send, recv_sem=recv,
            device_id={"patch": target}, device_id_type=MESH,
        )

    def along(h, source, target, send):
        where = held.at[h, slot(source)]
        return to_chip(where, where, send.at[h, source], line_recv.at[h, source], target)

    def aside(h, source):
        where = held.at[h, slot(source)]
        return pltpu.make_async_remote_copy(
            src_ref=where, dst_ref=where, send_sem=side_send.at[h, source],
            recv_sem=side_recv.at[h, source],
            device_id={"seq": other_core}, device_id_type=MESH,
        )

    def lend(h):
        return to_chip(
            query.at[h], guest.at[h], guest_send.at[h], guest_recv.at[h], inner
        )

    def give_back(h):
        return to_chip(
            mixed.at[h], returned.at[h], back_send.at[h], back_recv.at[h], outer
        )

    has_text = (chip == 0) & (side == 0)
    gives_text = (chip == 0) & (side == 1)
    text_rows = rows * 8 // TEXT_PART
    chunk = features // 2 // CHUNKS

    def weight_rows(owner, c):
        return pl.ds(pl.multiple_of(owner * (features // 2) + c * chunk, chunk), chunk)

    def across(stream, c):
        where = weight_rows(group, c)
        return pltpu.make_async_remote_copy(
            src_ref=weight.at[stream, where], dst_ref=far_weight.at[stream, where],
            send_sem=across_send.at[stream, c], recv_sem=across_recv.at[stream, c],
            device_id={"tensor": 1 - side}, device_id_type=MESH,
        )

    def pass_on(stream, c):
        where = far_weight.at[stream, weight_rows(group, c)]
        return pltpu.make_async_remote_copy(
            src_ref=where, dst_ref=where,
            send_sem=group_send.at[stream, c], recv_sem=group_recv.at[stream, c],
            device_id={"group": 1 - group}, device_id_type=MESH,
        )

    def relay(stream, c):
        across(stream, c).wait_recv()
        pass_on(stream, c).start()

    def load(stream):
        return pltpu.make_async_copy(
            weight.at[stream], own_weight.at[stream], load_sem.at[stream]
        )

    def hand_over(h, which):
        if which == 2:
            target = {"seq": other_core}
        else:
            target = {"tensor": 1 - side, "seq": core if which == 0 else other_core}
        return pltpu.make_async_remote_copy(
            src_ref=returned.at[h], dst_ref=full.at[side, h],
            send_sem=full_send.at[min(which, 1), h], recv_sem=full_recv.at[side, h],
            device_id=target, device_id_type=MESH,
        )

    def received(origin, h):
        where = full.at[origin, h]
        return pltpu.make_async_remote_copy(
            src_ref=where, dst_ref=where,
            send_sem=full_send.at[0, h], recv_sem=full_recv.at[origin, h],
            device_id={"seq": other_core}, device_id_type=MESH,
        )

    straight = side == core
    image_rows = pl.ds(text_rows, rows - text_rows)

    def lend_rows(h):
        return pltpu.make_async_remote_copy(
            src_ref=returned.at[h, image_rows], dst_ref=lent_rows.at[h],
            send_sem=lent_send.at[h], recv_sem=lent_recv.at[h],
            device_id={"seq": other_core}, device_id_type=MESH,
        )

    def send_part():
        return pltpu.make_async_remote_copy(
            src_ref=part_out, dst_ref=part_in,
            send_sem=part_sem.at[0], recv_sem=part_sem.at[1],
            device_id={"tensor": 1 - side}, device_id_type=MESH,
        )

    def distribute(h):
        @pl.when(straight)
        def _():
            hand_over(h, 2).start()
            full[side, h] = returned[h]

        @pl.when(jnp.logical_not(straight))
        def _():
            hand_over(h, 0).start()
            hand_over(h, 1).start()

        @pl.when(gives_text & (core == 0))
        def _():
            lend_rows(h).start()

    factor = hd ** (-0.5) * math.log2(math.e)

    def attend(rows_q, h):
        keys = held[h, :, 0].reshape(8 * rows, hd)
        values = held[h, :, 1].reshape(8 * rows, hd)
        values = jnp.concatenate([values, jnp.ones_like(values)], 1)
        half = rows // 2
        parts = []
        for start in (0, half):
            scores = lax.dot_general(
                rows_q[h, start : start + half],
                keys,
                (((1,), (1,)), ((), ())),
                preferred_element_type=jnp.float32,
            )
            weights = jnp.exp2(scores * factor).astype(jnp.bfloat16)
            total = jnp.dot(weights, values, preferred_element_type=jnp.float32)
            parts.append((total[:, :hd] / total[:, hd:]).astype(jnp.bfloat16))
        return jnp.concatenate(parts, 0)

    barrier = pltpu.get_barrier_semaphore()
    pl.semaphore_signal(barrier, inc=1, device_id={"seq": other_core}, device_id_type=MESH)
    pl.semaphore_signal(barrier, inc=1, device_id={"patch": inner}, device_id_type=MESH)

    for target in (
        {"group": 1 - group},
        {"tensor": 1 - side},
        {"tensor": 1 - side, "seq": other_core},
    ):
        pl.semaphore_signal(barrier, inc=1, device_id=target, device_id_type=MESH)

    @pl.when(is_mid)
    def _():
        pl.semaphore_signal(barrier, inc=1, device_id={"patch": outer}, device_id_type=MESH)

    row_ids = positions[:, 0:1]
    angle = row_ids * table[0:1, :] + positions[:, 1:2] * table[1:2, :]
    sine = jnp.sin(angle)
    cosine[...] = jnp.cos(angle)
    sine_low[...] = sine * table[2:3, :]
    sine_high[...] = sine * table[3:4, :]
    text = row_ids == 0
    gain_q[...] = jnp.where(text, gains[0:1, :], gains[2:3, :])
    gain_k[...] = jnp.where(text, gains[1:2, :], gains[3:4, :])

    full_mean = jnp.full((hd, hd), 1.0 / hd, jnp.float32)
    in_low = lax.broadcasted_iota(jnp.int32, (hd, hd), 0) < hd // 2
    out_low = lax.broadcasted_iota(jnp.int32, (hd, hd), 1) < hd // 2
    half_mean = jnp.where(in_low == out_low, 2.0 / hd, 0.0)
    half_len = RB // 2

    def prepare_head(h):
        place = pl.ds(pl.multiple_of(h * hd, hd), hd)
        whole = (sizes[h] == hd).astype(jnp.float32)
        grouped = (whole * full_mean + (1.0 - whole) * half_mean).astype(jnp.bfloat16)

        def embed(raw, gain):
            values = raw[:, place].astype(jnp.float32)
            mean_sq = split_dot(values * values, full_mean.astype(jnp.bfloat16))
            normed = values * lax.rsqrt(mean_sq + norm_eps) * gain[...]
            return (
                normed * cosine[...]
                + pltpu.roll(normed, hd - half_len, 1) * sine_low[...]
                + pltpu.roll(normed, half_len, 1) * sine_high[...]
            )

        def update(fresh, old):
            kept = old[:, place].astype(jnp.float32)
            residual = fresh - kept
            scale = jnp.sqrt(split_dot(residual * residual, grouped) + norm_eps)
            scale = scale.astype(jnp.bfloat16).astype(jnp.float32)
            code = jnp.tanh(residual / scale).astype(jnp.bfloat16).astype(jnp.float32)
            return (kept + scale * code).astype(jnp.bfloat16)

        key_next = update(embed(key_raw, gain_k), key_old)
        value_next = update(value_raw[:, place].astype(jnp.float32), value_old)
        held[h, slot(chip), 0] = key_next
        held[h, slot(chip), 1] = value_next
        key_out[:, place] = key_next
        value_out[:, place] = value_next
        query[h] = embed(query_raw, gain_q).astype(jnp.bfloat16)

    pl.semaphore_wait(barrier, jnp.where(is_end, 5, 6))

    def arrived(h, source):
        along(h, source, inner, in_send).wait_recv()

    def siblings(h):
        def one(source, carry):
            aside(h, source).wait_recv()
            return carry

        lax.fori_loop(0, 4, one, 0)

    def start_weights():
        for c in range(CHUNKS):
            @pl.when(gives_text)
            def _():
                across(0, c).start()

            @pl.when(jnp.logical_not(gives_text))
            def _():
                across(1, c).start()

        load(1).start()

        @pl.when(has_text)
        def _():
            load(0).start()

    start_weights()

    @pl.when(is_end)
    def _():
        def push(h, carry):
            prepare_head(h)
            along(h, chip, inner, in_send).start()

            @pl.when(h < shared)
            def _():
                aside(h, chip).start()

            @pl.when(h >= shared)
            def _():
                lend(h).start()

            return carry

        lax.fori_loop(0, heads, push, 0)

        def step(h, carry):
            for source in (my_mid, far_mid, far_end):
                arrived(h, source)
                aside(h, source).start()
            siblings(h)
            returned[h] = attend(query, h)
            distribute(h)

            @pl.when(has_text)
            def _():
                relay(0, h)

            @pl.when(jnp.logical_not(has_text))
            def _():
                relay(1, h)

            return carry

        lax.fori_loop(0, shared, step, 0)

        def finish(h, carry):
            give_back(h).wait_recv()
            distribute(h)
            return carry

        lax.fori_loop(shared, heads, finish, 0)

        def drain(h, carry):
            along(h, chip, inner, in_send).wait_send()

            @pl.when(h < shared)
            def _():
                for source in (chip, my_mid, far_mid, far_end):
                    aside(h, source).wait_send()

            @pl.when(h >= shared)
            def _():
                lend(h).wait_send()

            return carry

        lax.fori_loop(0, heads, drain, 0)

    @pl.when(is_mid)
    def _():
        def push(h, carry):
            prepare_head(h)
            @pl.when(h < 2)
            def _():
                along(h, chip, inner, in_send).start()

            @pl.when(h < shared)
            def _():
                along(h, chip, outer, out_send).start()

            aside(h, chip).start()
            return carry

        lax.fori_loop(0, heads, push, 0)

        def take_end(h):
            arrived(h, my_end)
            along(h, my_end, inner, in_send).start()
            aside(h, my_end).start()

        take_end(0)

        def step(h, carry):
            @pl.when(h + 2 < heads)
            def _():
                along(h + 2, chip, inner, in_send).start()

            @pl.when(h + 1 < heads)
            def _():
                take_end(h + 1)

            for source in (far_mid, far_end):
                arrived(h, source)
                aside(h, source).start()

                @pl.when(h < shared)
                def _():
                    along(h, source, outer, out_send).start()

            siblings(h)

            @pl.when(h >= shared)
            def _():
                lend(h).wait_recv()
                mixed[h] = attend(guest, h)
                give_back(h).start()

            returned[h] = attend(query, h)
            distribute(h)

            @pl.when(h < CHUNKS)
            def _():
                relay(1, h)

            return carry

        lax.fori_loop(0, heads, step, 0)

        def drain(h, carry):
            along(h, chip, inner, in_send).wait_send()
            along(h, my_end, inner, in_send).wait_send()
            for source in (chip, my_end, far_mid, far_end):
                aside(h, source).wait_send()

            @pl.when(h < shared)
            def _():
                for source in (chip, far_mid, far_end):
                    along(h, source, outer, out_send).wait_send()

            @pl.when(h >= shared)
            def _():
                give_back(h).wait_send()

            return carry

        lax.fori_loop(0, heads, drain, 0)

    width = 512
    load(1).wait()

    @pl.when(gives_text)
    def _():
        @pl.when(core == 0)
        def _():
            for h in range(heads):
                lent_rows[h] = returned[h, text_rows:]

        @pl.when(core == 1)
        def _():
            for h in range(heads):
                lend_rows(h).wait_recv()

        partial_rows = jnp.concatenate([lent_rows[h] for h in range(heads)], 1)
        for first in range(0, columns, width):
            part_out[:, first : first + width] = jnp.dot(
                partial_rows,
                own_weight[1, :, first : first + width],
                preferred_element_type=jnp.float32,
            ).astype(part_out.dtype)
        send_part().start()

    @pl.when(jnp.logical_not(has_text))
    def _():
        for c in range(CHUNKS):
            pass_on(1, c).wait_recv()

    @pl.when(has_text)
    def _():
        load(0).wait()
        for c in range(CHUNKS):
            pass_on(0, c).wait_recv()

    def collect(h, carry):
        received(1 - side, h).wait_recv()

        @pl.when(jnp.logical_not(straight))
        def _():
            received(side, h).wait_recv()

        return carry

    lax.fori_loop(0, heads, collect, 0)
    own_rows = jnp.concatenate([full[side, h] for h in range(heads)], 1)
    far_rows = jnp.concatenate([full[1 - side, h] for h in range(heads)], 1)
    def project(first, last, stream, place):
        sums = jnp.dot(
            own_rows[first:last], own_weight[stream, :, place], preferred_element_type=jnp.float32
        ) + jnp.dot(
            far_rows[first:last], far_weight[stream, :, place], preferred_element_type=jnp.float32
        )
        out[first:last, place] = (sums * gates[stream : stream + 1, place]).astype(out.dtype)

    def block(index, carry):
        place = pl.ds(pl.multiple_of(index * width, width), width)

        @pl.when(has_text)
        def _():
            project(0, text_rows, 0, place)

        @pl.when(jnp.logical_not(has_text))
        def _():
            project(0, rows, 1, place)

        return carry

    lax.fori_loop(0, columns // width, block, 0)

    @pl.when(has_text)
    def _():
        send_part().wait_recv()
        for first in range(0, columns, width):
            last = first + width
            sums = jnp.dot(
                own_rows[text_rows:], own_weight[1, :, first:last],
                preferred_element_type=jnp.float32,
            ) + part_in[:, first:last].astype(jnp.float32)
            out[text_rows:, first:last] = (sums * gates[1:2, first:last]).astype(out.dtype)

    def drain_rows(h, carry):
        @pl.when(straight)
        def _():
            hand_over(h, 2).wait_send()

        @pl.when(jnp.logical_not(straight))
        def _():
            hand_over(h, 0).wait_send()
            hand_over(h, 1).wait_send()

        return carry

    lax.fori_loop(0, heads, drain_rows, 0)
    for c in range(CHUNKS):
        @pl.when(gives_text)
        def _():
            across(0, c).wait_send()

        @pl.when(jnp.logical_not(gives_text))
        def _():
            across(1, c).wait_send()

        @pl.when(has_text)
        def _():
            pass_on(0, c).wait_send()

        @pl.when(jnp.logical_not(has_text))
        def _():
            pass_on(1, c).wait_send()

    @pl.when(gives_text)
    def _():
        send_part().wait_send()

        @pl.when(core == 0)
        def _():
            for h in range(heads):
                lend_rows(h).wait_send()


def on_device_line(
    query_raw,
    key_raw,
    value_raw,
    key_cache,
    value_cache,
    norm_gain,
    layout,
    group_size,
    step_index,
    gate_table,
    out_weight,
):
    rows, features = query_raw.shape
    heads = group_size.shape[0]
    hd = features // heads
    text_rows = rows * 8 // TEXT_PART
    dma = pltpu.SemaphoreType.DMA
    in_vmem = pl.BlockSpec(memory_space=pltpu.VMEM)
    in_smem = pl.BlockSpec(memory_space=pltpu.SMEM)
    vmem = lambda *shape: pltpu.VMEM(shape, jnp.bfloat16)
    wide = pltpu.VMEM((rows, hd), jnp.float32)
    return pl.pallas_call(
        attend_kernel,
        out_shape=[
            jax.ShapeDtypeStruct((rows, out_weight.shape[2]), jnp.bfloat16),
            jax.ShapeDtypeStruct((rows, features), jnp.bfloat16),
            jax.ShapeDtypeStruct((rows, features), jnp.bfloat16),
        ],
        in_specs=[in_smem] + [in_vmem] * 9 + [pl.BlockSpec(memory_space=pl.ANY)],
        out_specs=[in_vmem] * 3,
        scratch_shapes=[
            vmem(heads, rows, hd),
        ]
        + [wide] * 5
        + [
            vmem(heads, 8, 2, rows, hd),
            vmem(heads, rows, hd),
            vmem(heads, rows, hd),
            vmem(heads, rows, hd),
            vmem(2, heads, rows, hd),
            vmem(*out_weight.shape),
            vmem(*out_weight.shape),
        ]
        + [dma((heads, 4))] * 5
        + [dma((heads,))] * 4
        + [dma((2, heads))] * 2
        + [dma((2, CHUNKS))] * 4
        + [dma((2,))]
        + [
            vmem(heads, rows - text_rows, hd),
            vmem(rows - text_rows, out_weight.shape[2]),
            vmem(rows - text_rows, out_weight.shape[2]),
        ]
        + [dma((heads,))] * 2
        + [dma((2,))],
        compiler_params=pltpu.CompilerParams(
            collective_id=0, has_side_effects=True, vmem_limit_bytes=60 * 2**20
        ),
    )(
        group_size,
        layout.astype(jnp.float32).T,
        norm_gain.reshape(4, hd),
        lane_tables(hd),
        query_raw,
        key_raw,
        value_raw,
        key_cache,
        value_cache,
        lax.dynamic_index_in_dim(gate_table, step_index[0], 1, keepdims=False),
        out_weight,
    )


def solution(mesh):
    in_specs = (
        P(("group", "patch", "seq"), "tensor"),
        P(("group", "patch", "seq"), "tensor"),
        P(("group", "patch", "seq"), "tensor"),
        P(("group", "patch", "seq"), "tensor"),
        P(("group", "patch", "seq"), "tensor"),
        P(),
        P(None, ("group", "patch", "seq")),
        P("tensor"),
        P("group"),
        P(None, None, "seq"),
        P(None, "tensor", "seq"),
    )
    out_specs = (
        P(("group", "patch", "tensor"), "seq"),
        P(("group", "patch", "seq"), "tensor"),
        P(("group", "patch", "seq"), "tensor"),
    )
    fast = mesh.shape["patch"] == 4 and mesh.shape["tensor"] == 2 and mesh.shape["seq"] == 2
    return jax.shard_map(
        on_device_line if fast else on_device, mesh=mesh, in_specs=in_specs, out_specs=out_specs, check_vma=False
    )
```

```python
import functools
import math
import jax
import jax.numpy as jnp
import numpy as np
from jax import lax
from jax.experimental import pallas as pl
from jax.experimental.pallas import tpu as pltpu
from jax.sharding import PartitionSpec as P

RA = 16
RB = 56


rope_theta = 10000.0
norm_eps = 1e-06


def rope_tables(positions, plain_dims, rotary_dims):
    half_len = rotary_dims // 2
    exponent = jnp.arange(half_len, dtype=jnp.float32) * (2.0 / rotary_dims)
    freqs = jnp.exp(-jnp.log(rope_theta) * exponent)
    token_count = positions.shape[1]
    cosine = [jnp.ones((token_count, plain_dims), jnp.float32)]
    sine_part = [jnp.zeros((token_count, plain_dims), jnp.float32)]
    for which in range(2):
        angle = positions[which].astype(jnp.float32)[:, None] * freqs[None, :]
        cosine += [jnp.cos(angle), jnp.cos(angle)]
        sine_part += [jnp.sin(angle), jnp.sin(angle)]
    return (jnp.concatenate(cosine, 1), jnp.concatenate(sine_part, 1))


def partner(values, plain_dims, rotary_dims):
    half_len = rotary_dims // 2
    second = plain_dims + rotary_dims
    return jnp.concatenate(
        [
            values[..., :plain_dims],
            -values[..., plain_dims + half_len : second],
            values[..., plain_dims : plain_dims + half_len],
            -values[..., second + half_len :],
            values[..., second : second + half_len],
        ],
        -1,
    )


def compress(residual, group_size, heads, head_dim):
    row_count = residual.shape[0]
    halves = residual.reshape(row_count, heads, 2, head_dim // 2)
    half_ms = jnp.mean(halves * halves, -1)
    whole_ms = jnp.mean(half_ms, -1, keepdims=True)
    whole = (group_size == head_dim)[None, :, None]
    mean_sq = jnp.where(whole, whole_ms, half_ms)
    scales = jnp.sqrt(mean_sq + norm_eps).astype(jnp.bfloat16)
    codes = jnp.tanh(halves / scales.astype(jnp.float32)[..., None]).astype(jnp.bfloat16)
    return (codes.reshape(row_count, heads * head_dim), scales.reshape(row_count, heads * 2))


def decode(codes, scales, heads, head_dim):
    row_count = codes.shape[0]
    parts = codes.astype(jnp.float32).reshape(row_count, heads, 2, head_dim // 2) * scales.astype(
        jnp.float32
    ).reshape(row_count, heads, 2, 1)
    return parts.reshape(row_count, heads * head_dim)


def prepare(query_raw, key_raw, value_raw, positions, norm_gain, key_rows, value_rows, group_size):
    row_count = query_raw.shape[0]
    heads = group_size.shape[0]
    head_dim = norm_gain.shape[-1]
    text_rows = (positions[0] == 0)[:, None, None]
    cosine, sine_part = rope_tables(positions, RA, RB)
    cosine = cosine[:, None, :]
    sine_part = sine_part[:, None, :]

    def embed(raw, which):
        gain = jnp.where(
            text_rows, norm_gain[0, which][None, None, :], norm_gain[1, which][None, None, :]
        )
        values = raw.astype(jnp.float32).reshape(row_count, heads, head_dim)
        normed = values * lax.rsqrt(jnp.mean(values * values, -1, keepdims=True) + norm_eps) * gain
        return (normed * cosine + partner(normed, RA, RB) * sine_part).reshape(
            row_count, heads * head_dim
        )

    query_rot = embed(query_raw, 0).astype(jnp.bfloat16)
    key_rot = embed(key_raw, 1)
    key_codes, key_scales = compress(
        key_rot - key_rows.astype(jnp.float32), group_size, heads, head_dim
    )
    value_codes, value_scales = compress(
        value_raw.astype(jnp.float32) - value_rows.astype(jnp.float32), group_size, heads, head_dim
    )
    return (query_rot, key_codes, value_codes, key_scales, value_scales)


def block_length(piece_rows):
    for candidate in range(min(piece_rows, 2048), 0, -1):
        if piece_rows % candidate == 0:
            return candidate
    return piece_rows


def on_device(
    query_raw,
    key_raw,
    value_raw,
    key_cache,
    value_cache,
    norm_gain,
    layout,
    group_size,
    step_index,
    gate_table,
    out_weight,
):
    row_count = query_raw.shape[0]
    heads = group_size.shape[0]
    head_dim = norm_gain.shape[-1]
    query_rot, key_codes, value_codes, key_scales, value_scales = prepare(
        query_raw, key_raw, value_raw, layout, norm_gain, key_cache, value_cache, group_size
    )
    key_mine = (
        key_cache.astype(jnp.float32) + decode(key_codes, key_scales, heads, head_dim)
    ).astype(jnp.bfloat16)
    value_mine = (
        value_cache.astype(jnp.float32) + decode(value_codes, value_scales, heads, head_dim)
    ).astype(jnp.bfloat16)
    query_heads = query_rot.reshape(row_count, heads, head_dim)
    inverse_root = head_dim ** (-0.5)
    start_state = (
        jnp.zeros((heads, row_count, head_dim), jnp.float32),
        jnp.zeros((heads, row_count), jnp.float32),
    )
    keys_all = lax.all_gather(key_mine, ("patch", "seq"), axis=0, tiled=True)
    values_all = lax.all_gather(value_mine, ("patch", "seq"), axis=0, tiled=True)
    piece_rows = keys_all.shape[0]
    length = block_length(piece_rows)

    def one_block(index, carry):
        numer, totals = carry
        keys = lax.dynamic_slice_in_dim(keys_all, index * length, length, 0).reshape(
            length, heads, head_dim
        )
        values = lax.dynamic_slice_in_dim(values_all, index * length, length, 0).reshape(
            length, heads, head_dim
        )
        scores = (
            jnp.einsum("qhd,khd->hqk", query_heads, keys, preferred_element_type=jnp.float32)
            * inverse_root
        )
        weights = jnp.exp(scores)
        totals = totals + jnp.sum(weights, -1)
        numer = numer + jnp.einsum(
            "hqk,khd->hqd", weights.astype(jnp.bfloat16), values, preferred_element_type=jnp.float32
        )
        return (numer, totals)

    numer, totals = lax.fori_loop(0, piece_rows // length, one_block, start_state)
    attn_rows = (
        (numer / totals[..., None])
        .transpose(1, 0, 2)
        .reshape(row_count, heads * head_dim)
        .astype(jnp.bfloat16)
    )
    text_flag = (layout[0] == 0).astype(jnp.bfloat16)
    pair_attn, pair_text = (
        lax.all_gather(attn_rows, "seq", axis=0, tiled=True),
        lax.all_gather(text_flag, "seq", axis=0, tiled=True),
    )
    share = pair_attn.shape[0] // lax.axis_size("tensor")

    def both_streams(block, block_text):
        text_part = jnp.dot(block, out_weight[0], preferred_element_type=jnp.float32)
        image_part = jnp.dot(block, out_weight[1], preferred_element_type=jnp.float32)
        return jnp.where(block_text[:, None] > 0, text_part, image_part)

    def image_only(block, block_text):
        return jnp.dot(block, out_weight[1], preferred_element_type=jnp.float32)

    block = pair_attn
    block_text = pair_text
    projected = lax.psum_scatter(
        lax.cond(jnp.any(block_text > 0), both_streams, image_only, block, block_text),
        "tensor",
        scatter_dimension=0,
        tiled=True,
    )
    mine_text = lax.dynamic_slice_in_dim(pair_text, lax.axis_index("tensor") * share, share, 0)
    chosen = (jnp.arange(gate_table.shape[1]) == step_index[0]).astype(jnp.float32)
    gates = jnp.sum(gate_table * chosen[None, :, None], 1)
    gate_rows = jnp.where(mine_text[:, None] > 0, gates[0][None, :], gates[1][None, :])
    return ((gate_rows * projected).astype(jnp.bfloat16), key_mine, value_mine)


MESH = pl.DeviceIdType.MESH
GATHER_SHARE = 2
CHUNKS = 3
TEXT_PART = 12


def lane_tables(head_dim):
    half_len = RB // 2
    freqs = np.exp(-math.log(rope_theta) * np.arange(half_len) * (2.0 / RB)).astype(np.float32)
    table = np.zeros((8, head_dim), np.float32)
    for which in range(2):
        start = RA + which * RB
        table[which, start : start + half_len] = freqs
        table[which, start + half_len : start + RB] = freqs
        table[2, start : start + half_len] = -1.0
        table[3, start + half_len : start + RB] = 1.0
    return jnp.asarray(table)


def split_dot(values, matrix):
    high = values.astype(jnp.bfloat16)
    low = (values - high.astype(jnp.float32)).astype(jnp.bfloat16)
    return jnp.dot(
        jnp.concatenate([high, low], 1),
        jnp.concatenate([matrix, matrix], 0),
        preferred_element_type=jnp.float32,
    )


def attend_kernel(
    sizes, positions, gains, table, query_raw, key_raw, value_raw, key_old, value_old,
    gates, weight, out, key_out, value_out, query, cosine, sine_low, sine_high,
    gain_q, gain_k, held, guest, mixed, returned, full, own_weight, far_weight,
    in_send, out_send, side_send, line_recv, side_recv, guest_send, guest_recv, back_send,
    back_recv, full_send, full_recv, across_send, across_recv, group_send, group_recv, load_sem,
    lent_rows, part_out, part_in, lent_send, lent_recv, part_sem,
):
    heads, rows, hd = query.shape
    features, columns = weight.shape[1:]
    group = lax.axis_index("group")
    side = lax.axis_index("tensor")
    shared = heads // GATHER_SHARE
    chip = lax.axis_index("patch")
    core = lax.axis_index("seq")
    other_core = 1 - core
    upper = chip // 2
    is_end = (chip == 0) | (chip == 3)
    is_mid = jnp.logical_not(is_end)
    my_end = upper * 3
    my_mid = 1 + upper
    far_mid = 2 - upper
    far_end = 3 - my_end
    inner = jnp.where(is_end, my_mid, far_mid)
    outer = my_end

    def slot(source):
        return source * 2 + core

    def to_chip(src, dst, send, recv, target):
        return pltpu.make_async_remote_copy(
            src_ref=src, dst_ref=dst, send_sem=send, recv_sem=recv,
            device_id={"patch": target}, device_id_type=MESH,
        )

    def along(h, source, target, send):
        where = held.at[h, slot(source)]
        return to_chip(where, where, send.at[h, source], line_recv.at[h, source], target)

    def aside(h, source):
        where = held.at[h, slot(source)]
        return pltpu.make_async_remote_copy(
            src_ref=where, dst_ref=where, send_sem=side_send.at[h, source],
            recv_sem=side_recv.at[h, source],
            device_id={"seq": other_core}, device_id_type=MESH,
        )

    def lend(h):
        return to_chip(
            query.at[h], guest.at[h], guest_send.at[h], guest_recv.at[h], inner
        )

    def give_back(h):
        return to_chip(
            mixed.at[h], returned.at[h], back_send.at[h], back_recv.at[h], outer
        )

    has_text = (chip == 0) & (side == 0)
    gives_text = (chip == 0) & (side == 1)
    text_rows = rows * 8 // TEXT_PART
    chunk = features // 2 // CHUNKS

    def weight_rows(owner, c):
        return pl.ds(pl.multiple_of(owner * (features // 2) + c * chunk, chunk), chunk)

    def across(stream, c):
        where = weight_rows(group, c)
        return pltpu.make_async_remote_copy(
            src_ref=weight.at[stream, where], dst_ref=far_weight.at[stream, where],
            send_sem=across_send.at[stream, c], recv_sem=across_recv.at[stream, c],
            device_id={"tensor": 1 - side}, device_id_type=MESH,
        )

    def pass_on(stream, c):
        where = far_weight.at[stream, weight_rows(group, c)]
        return pltpu.make_async_remote_copy(
            src_ref=where, dst_ref=where,
            send_sem=group_send.at[stream, c], recv_sem=group_recv.at[stream, c],
            device_id={"group": 1 - group}, device_id_type=MESH,
        )

    def relay(stream, c):
        across(stream, c).wait_recv()
        pass_on(stream, c).start()

    def load(stream):
        return pltpu.make_async_copy(
            weight.at[stream], own_weight.at[stream], load_sem.at[stream]
        )

    def hand_over(h, which):
        if which == 2:
            target = {"seq": other_core}
        else:
            target = {"tensor": 1 - side, "seq": core if which == 0 else other_core}
        return pltpu.make_async_remote_copy(
            src_ref=returned.at[h], dst_ref=full.at[side, h],
            send_sem=full_send.at[min(which, 1), h], recv_sem=full_recv.at[side, h],
            device_id=target, device_id_type=MESH,
        )

    def received(origin, h):
        where = full.at[origin, h]
        return pltpu.make_async_remote_copy(
            src_ref=where, dst_ref=where,
            send_sem=full_send.at[0, h], recv_sem=full_recv.at[origin, h],
            device_id={"seq": other_core}, device_id_type=MESH,
        )

    straight = side == core
    width = 512
    image_rows = pl.ds(text_rows, rows - text_rows)

    def lend_rows(h):
        return pltpu.make_async_remote_copy(
            src_ref=returned.at[h, image_rows], dst_ref=lent_rows.at[h],
            send_sem=lent_send.at[h], recv_sem=lent_recv.at[h],
            device_id={"seq": other_core}, device_id_type=MESH,
        )

    def send_part(first):
        place = pl.ds(first, width)
        return pltpu.make_async_remote_copy(
            src_ref=part_out.at[:, place], dst_ref=part_in.at[:, place],
            send_sem=part_sem.at[0, first // width], recv_sem=part_sem.at[1, first // width],
            device_id={"tensor": 1 - side}, device_id_type=MESH,
        )

    def distribute(h):
        @pl.when(straight)
        def _():
            hand_over(h, 2).start()
            full[side, h] = returned[h]

        @pl.when(jnp.logical_not(straight))
        def _():
            hand_over(h, 0).start()
            hand_over(h, 1).start()

        @pl.when(gives_text & (core == 0))
        def _():
            lend_rows(h).start()

    factor = hd ** (-0.5) * math.log2(math.e)

    def attend(rows_q, h):
        keys = held[h, :, 0].reshape(8 * rows, hd)
        values = held[h, :, 1].reshape(8 * rows, hd)
        values = jnp.concatenate([values, jnp.ones_like(values)], 1)
        half = rows // 2
        parts = []
        for start in (0, half):
            scores = lax.dot_general(
                rows_q[h, start : start + half],
                keys,
                (((1,), (1,)), ((), ())),
                preferred_element_type=jnp.float32,
            )
            weights = jnp.exp2(scores * factor).astype(jnp.bfloat16)
            total = jnp.dot(weights, values, preferred_element_type=jnp.float32)
            parts.append((total[:, :hd] / total[:, hd:]).astype(jnp.bfloat16))
        return jnp.concatenate(parts, 0)

    barrier = pltpu.get_barrier_semaphore()
    pl.semaphore_signal(barrier, inc=1, device_id={"seq": other_core}, device_id_type=MESH)
    pl.semaphore_signal(barrier, inc=1, device_id={"patch": inner}, device_id_type=MESH)

    for target in (
        {"group": 1 - group},
        {"tensor": 1 - side},
        {"tensor": 1 - side, "seq": other_core},
    ):
        pl.semaphore_signal(barrier, inc=1, device_id=target, device_id_type=MESH)

    @pl.when(is_mid)
    def _():
        pl.semaphore_signal(barrier, inc=1, device_id={"patch": outer}, device_id_type=MESH)

    row_ids = positions[:, 0:1]
    angle = row_ids * table[0:1, :] + positions[:, 1:2] * table[1:2, :]
    sine = jnp.sin(angle)
    cosine[...] = jnp.cos(angle)
    sine_low[...] = sine * table[2:3, :]
    sine_high[...] = sine * table[3:4, :]
    text = row_ids == 0
    gain_q[...] = jnp.where(text, gains[0:1, :], gains[2:3, :])
    gain_k[...] = jnp.where(text, gains[1:2, :], gains[3:4, :])

    full_mean = jnp.full((hd, hd), 1.0 / hd, jnp.float32)
    in_low = lax.broadcasted_iota(jnp.int32, (hd, hd), 0) < hd // 2
    out_low = lax.broadcasted_iota(jnp.int32, (hd, hd), 1) < hd // 2
    half_mean = jnp.where(in_low == out_low, 2.0 / hd, 0.0)
    half_len = RB // 2

    def prepare_head(h):
        place = pl.ds(pl.multiple_of(h * hd, hd), hd)
        whole = (sizes[h] == hd).astype(jnp.float32)
        grouped = (whole * full_mean + (1.0 - whole) * half_mean).astype(jnp.bfloat16)

        def embed(raw, gain):
            values = raw[:, place].astype(jnp.float32)
            mean_sq = split_dot(values * values, full_mean.astype(jnp.bfloat16))
            normed = values * lax.rsqrt(mean_sq + norm_eps) * gain[...]
            return (
                normed * cosine[...]
                + pltpu.roll(normed, hd - half_len, 1) * sine_low[...]
                + pltpu.roll(normed, half_len, 1) * sine_high[...]
            )

        def update(fresh, old):
            kept = old[:, place].astype(jnp.float32)
            residual = fresh - kept
            scale = jnp.sqrt(split_dot(residual * residual, grouped) + norm_eps)
            scale = scale.astype(jnp.bfloat16).astype(jnp.float32)
            code = jnp.tanh(residual / scale).astype(jnp.bfloat16).astype(jnp.float32)
            return (kept + scale * code).astype(jnp.bfloat16)

        key_next = update(embed(key_raw, gain_k), key_old)
        value_next = update(value_raw[:, place].astype(jnp.float32), value_old)
        held[h, slot(chip), 0] = key_next
        held[h, slot(chip), 1] = value_next
        key_out[:, place] = key_next
        value_out[:, place] = value_next
        query[h] = embed(query_raw, gain_q).astype(jnp.bfloat16)

    pl.semaphore_wait(barrier, jnp.where(is_end, 5, 6))

    def arrived(h, source):
        along(h, source, inner, in_send).wait_recv()

    def siblings(h):
        def one(source, carry):
            aside(h, source).wait_recv()
            return carry

        lax.fori_loop(0, 4, one, 0)

    def start_weights():
        for c in range(CHUNKS):
            @pl.when(gives_text)
            def _():
                across(0, c).start()

            @pl.when(jnp.logical_not(gives_text))
            def _():
                across(1, c).start()

        load(1).start()

        @pl.when(has_text)
        def _():
            load(0).start()

    start_weights()

    @pl.when(is_end)
    def _():
        def push(h, carry):
            prepare_head(h)
            along(h, chip, inner, in_send).start()

            @pl.when(h < shared)
            def _():
                aside(h, chip).start()

            @pl.when(h >= shared)
            def _():
                lend(h).start()

            return carry

        lax.fori_loop(0, heads, push, 0)

        def step(h, carry):
            for source in (my_mid, far_mid, far_end):
                arrived(h, source)
                aside(h, source).start()
            siblings(h)
            returned[h] = attend(query, h)
            distribute(h)

            @pl.when(has_text)
            def _():
                relay(0, h)

            @pl.when(jnp.logical_not(has_text))
            def _():
                relay(1, h)

            return carry

        lax.fori_loop(0, shared, step, 0)

        def finish(h, carry):
            give_back(h).wait_recv()
            distribute(h)
            return carry

        lax.fori_loop(shared, heads, finish, 0)

        def drain(h, carry):
            along(h, chip, inner, in_send).wait_send()

            @pl.when(h < shared)
            def _():
                for source in (chip, my_mid, far_mid, far_end):
                    aside(h, source).wait_send()

            @pl.when(h >= shared)
            def _():
                lend(h).wait_send()

            return carry

        lax.fori_loop(0, heads, drain, 0)

    @pl.when(is_mid)
    def _():
        def push(h, carry):
            prepare_head(h)
            @pl.when(h < 2)
            def _():
                along(h, chip, inner, in_send).start()

            @pl.when(h < shared)
            def _():
                along(h, chip, outer, out_send).start()

            aside(h, chip).start()
            return carry

        lax.fori_loop(0, heads, push, 0)

        def take_end(h):
            arrived(h, my_end)
            along(h, my_end, inner, in_send).start()
            aside(h, my_end).start()

        take_end(0)

        def step(h, carry):
            @pl.when(h + 2 < heads)
            def _():
                along(h + 2, chip, inner, in_send).start()

            @pl.when(h + 1 < heads)
            def _():
                take_end(h + 1)

            for source in (far_mid, far_end):
                arrived(h, source)
                aside(h, source).start()

                @pl.when(h < shared)
                def _():
                    along(h, source, outer, out_send).start()

            siblings(h)

            @pl.when(h >= shared)
            def _():
                lend(h).wait_recv()
                mixed[h] = attend(guest, h)
                give_back(h).start()

            returned[h] = attend(query, h)
            distribute(h)

            @pl.when(h < CHUNKS)
            def _():
                relay(1, h)

            return carry

        lax.fori_loop(0, heads, step, 0)

        def drain(h, carry):
            along(h, chip, inner, in_send).wait_send()
            along(h, my_end, inner, in_send).wait_send()
            for source in (chip, my_end, far_mid, far_end):
                aside(h, source).wait_send()

            @pl.when(h < shared)
            def _():
                for source in (chip, far_mid, far_end):
                    along(h, source, outer, out_send).wait_send()

            @pl.when(h >= shared)
            def _():
                give_back(h).wait_send()

            return carry

        lax.fori_loop(0, heads, drain, 0)

    load(1).wait()

    @pl.when(gives_text)
    def _():
        @pl.when(core == 0)
        def _():
            for h in range(heads):
                lent_rows[h] = returned[h, text_rows:]

        @pl.when(core == 1)
        def _():
            for h in range(heads):
                lend_rows(h).wait_recv()

        partial_rows = jnp.concatenate([lent_rows[h] for h in range(heads)], 1)
        for first in range(0, columns, width):
            part_out[:, first : first + width] = jnp.dot(
                partial_rows,
                own_weight[1, :, first : first + width],
                preferred_element_type=jnp.float32,
            ).astype(part_out.dtype)
            send_part(first).start()

    @pl.when(jnp.logical_not(has_text))
    def _():
        for c in range(CHUNKS):
            pass_on(1, c).wait_recv()

    @pl.when(has_text)
    def _():
        load(0).wait()
        for c in range(CHUNKS):
            pass_on(0, c).wait_recv()

    def collect(h, carry):
        received(1 - side, h).wait_recv()

        @pl.when(jnp.logical_not(straight))
        def _():
            received(side, h).wait_recv()

        return carry

    lax.fori_loop(0, heads, collect, 0)
    own_rows = jnp.concatenate([full[side, h] for h in range(heads)], 1)
    far_rows = jnp.concatenate([full[1 - side, h] for h in range(heads)], 1)
    def project(first, last, stream, place):
        sums = jnp.dot(
            own_rows[first:last], own_weight[stream, :, place], preferred_element_type=jnp.float32
        ) + jnp.dot(
            far_rows[first:last], far_weight[stream, :, place], preferred_element_type=jnp.float32
        )
        out[first:last, place] = (sums * gates[stream : stream + 1, place]).astype(out.dtype)

    def block(index, carry):
        place = pl.ds(pl.multiple_of(index * width, width), width)

        @pl.when(has_text)
        def _():
            project(0, text_rows, 0, place)

        @pl.when(jnp.logical_not(has_text))
        def _():
            project(0, rows, 1, place)

        return carry

    lax.fori_loop(0, columns // width, block, 0)

    @pl.when(has_text)
    def _():
        for first in range(0, columns, width):
            send_part(first).wait_recv()
            last = first + width
            sums = jnp.dot(
                own_rows[text_rows:], own_weight[1, :, first:last],
                preferred_element_type=jnp.float32,
            ) + part_in[:, first:last].astype(jnp.float32)
            out[text_rows:, first:last] = (sums * gates[1:2, first:last]).astype(out.dtype)

    def drain_rows(h, carry):
        @pl.when(straight)
        def _():
            hand_over(h, 2).wait_send()

        @pl.when(jnp.logical_not(straight))
        def _():
            hand_over(h, 0).wait_send()
            hand_over(h, 1).wait_send()

        return carry

    lax.fori_loop(0, heads, drain_rows, 0)
    for c in range(CHUNKS):
        @pl.when(gives_text)
        def _():
            across(0, c).wait_send()

        @pl.when(jnp.logical_not(gives_text))
        def _():
            across(1, c).wait_send()

        @pl.when(has_text)
        def _():
            pass_on(0, c).wait_send()

        @pl.when(jnp.logical_not(has_text))
        def _():
            pass_on(1, c).wait_send()

    @pl.when(gives_text)
    def _():
        for first in range(0, columns, width):
            send_part(first).wait_send()

        @pl.when(core == 0)
        def _():
            for h in range(heads):
                lend_rows(h).wait_send()


def on_device_line(
    query_raw,
    key_raw,
    value_raw,
    key_cache,
    value_cache,
    norm_gain,
    layout,
    group_size,
    step_index,
    gate_table,
    out_weight,
):
    rows, features = query_raw.shape
    heads = group_size.shape[0]
    hd = features // heads
    text_rows = rows * 8 // TEXT_PART
    dma = pltpu.SemaphoreType.DMA
    in_vmem = pl.BlockSpec(memory_space=pltpu.VMEM)
    in_smem = pl.BlockSpec(memory_space=pltpu.SMEM)
    vmem = lambda *shape: pltpu.VMEM(shape, jnp.bfloat16)
    wide = pltpu.VMEM((rows, hd), jnp.float32)
    return pl.pallas_call(
        attend_kernel,
        out_shape=[
            jax.ShapeDtypeStruct((rows, out_weight.shape[2]), jnp.bfloat16),
            jax.ShapeDtypeStruct((rows, features), jnp.bfloat16),
            jax.ShapeDtypeStruct((rows, features), jnp.bfloat16),
        ],
        in_specs=[in_smem] + [in_vmem] * 9 + [pl.BlockSpec(memory_space=pl.ANY)],
        out_specs=[in_vmem] * 3,
        scratch_shapes=[
            vmem(heads, rows, hd),
        ]
        + [wide] * 5
        + [
            vmem(heads, 8, 2, rows, hd),
            vmem(heads, rows, hd),
            vmem(heads, rows, hd),
            vmem(heads, rows, hd),
            vmem(2, heads, rows, hd),
            vmem(*out_weight.shape),
            vmem(*out_weight.shape),
        ]
        + [dma((heads, 4))] * 5
        + [dma((heads,))] * 4
        + [dma((2, heads))] * 2
        + [dma((2, CHUNKS))] * 4
        + [dma((2,))]
        + [
            vmem(heads, rows - text_rows, hd),
            vmem(rows - text_rows, out_weight.shape[2]),
            vmem(rows - text_rows, out_weight.shape[2]),
        ]
        + [dma((heads,))] * 2
        + [dma((2, out_weight.shape[2] // 512))],
        compiler_params=pltpu.CompilerParams(
            collective_id=0, has_side_effects=True, vmem_limit_bytes=60 * 2**20
        ),
    )(
        group_size,
        layout.astype(jnp.float32).T,
        norm_gain.reshape(4, hd),
        lane_tables(hd),
        query_raw,
        key_raw,
        value_raw,
        key_cache,
        value_cache,
        lax.dynamic_index_in_dim(gate_table, step_index[0], 1, keepdims=False),
        out_weight,
    )


def solution(mesh):
    in_specs = (
        P(("group", "patch", "seq"), "tensor"),
        P(("group", "patch", "seq"), "tensor"),
        P(("group", "patch", "seq"), "tensor"),
        P(("group", "patch", "seq"), "tensor"),
        P(("group", "patch", "seq"), "tensor"),
        P(),
        P(None, ("group", "patch", "seq")),
        P("tensor"),
        P("group"),
        P(None, None, "seq"),
        P(None, "tensor", "seq"),
    )
    out_specs = (
        P(("group", "patch", "tensor"), "seq"),
        P(("group", "patch", "seq"), "tensor"),
        P(("group", "patch", "seq"), "tensor"),
    )
    fast = mesh.shape["patch"] == 4 and mesh.shape["tensor"] == 2 and mesh.shape["seq"] == 2
    return jax.shard_map(
        on_device_line if fast else on_device, mesh=mesh, in_specs=in_specs, out_specs=out_specs, check_vma=False
    )
```
